128 devices in a mesh: face: 8 (over y, core), tile: 16 (over z, x).
Axes of the slice: x: 4, y: 4, z: 4, core: 2. Of those that a mesh axis runs over, the one named last changes fastest.
Arguments:
- atm_tangent: float32 [64, 1048576], P(None, ('face', 'tile')), may hold values from -6 to 6
- atm_mixing: bfloat16 [63, 1048576], P(None, ('face', 'tile')), may hold values from 0.049804688 to 0.23925781
- flux_coef: float32 [4, 64], replicated, may hold values from -0.75 to 0.75
- remap_weight: bfloat16 [32768, 128, 128], P(('face', 'tile')), may hold values from -0.5 to 0.5
- target_device: int32 [8192, 4], P(('face', 'tile')), may hold values from 0 to 127, all different within a row; in each aligned block of 64 rows (0 to 63, 64 to 127, ...) at most 4 rows name the same one
- target_row: int32 [8192, 4], P(('face', 'tile')), may hold values from 0 to 63
- ocean_tangent: float32 [75, 512, 2048], P(None, 'face', 'tile'), may hold values from -6 to 6
- ocean_mixing: float32 [74], replicated, may hold values from 0.02 to 0.2
- penetration: float32 [75, 4], replicated, may hold values from -0.75 to 0.75
- sea_mask: int32 [512, 2048], P('face', 'tile'), may hold values 0 or 1
- ocean_adjoint: float32 [75, 512, 2048], P(None, 'face', 'tile'), may hold values from -6 to 6
Outputs:
- ocean_forward: float32 [75, 512, 2048], P(None, 'face', 'tile')
- ocean_backward: float32 [75, 512, 2048], P(None, 'face', 'tile')
- atm_adjoint: float32 [64, 1048576], P(None, ('face', 'tile'))
The draws below stay inside these ranges and needn't reach their ends.
Inputs may be any that keep to these rules, and one draw needn't show every extreme that they name: `target_device`: among one device's intersections no device is named more than 4 times; in every draw some device's intersections name one device exactly 4 times; the 4 devices of one block differ.
All inputs are finite; a program needn't handle non-finite values. No bound on the sum of `sea_mask` on one device may be relied on, other than what follows from the above.
Results may differ from the reference program's by a relative error of at most 0.0003.
Values sent between devices are 32-bit elements; how exact they have to be, the bound alone decides.
No kernel may reach another device: no remote copies, remote signals or barrier semaphores. Data moves between devices by JAX's collectives and lax.ppermute only.
A program may use at most 128 MiB of HBM per device.

```python
import math
import jax
import jax.numpy as jnp
import numpy as np
from jax import lax

LA = 64
LO = 75
FLD = 4
B = 128
NBA = 64
KO = 4
OY = 64
ATM_SWEEPS = 4
OCEAN_STEPS = 2
CAP = 4
BLOCKS = 8192
ATM_CELLS = 1048576
NY = 512
NX = 2048
N_FACE = 8
N_TILE = 16
DEVICES = 128


def with_ends(entries, rng, least, high):
    longest = entries.shape.index(max(entries.shape))
    spots = []
    for shift in (0, 1):
        where = [jax.random.randint(jax.random.fold_in(rng, axis), (), 0, length) for axis, length in enumerate(entries.shape)]
        where[longest] = (where[longest] + shift) % entries.shape[longest]
        spots.append(tuple(where))
    return entries.at[spots[0]].set(least).at[spots[1]].set(high)


def block_scale(stream_key, extent, shards, low, high):
    loudness, own = 1.0, jax.random.fold_in(stream_key, 6)
    for axis_at, blocks in shards:
        heights = jnp.exp(jax.random.uniform(jax.random.fold_in(own, axis_at), (blocks,), jnp.float32, low / len(shards), high / len(shards)))
        loudness = loudness * jnp.repeat(heights, extent[axis_at] // blocks).reshape([-1 if axis == axis_at else 1 for axis in range(len(extent))])
    return loudness


def deal_out(key, own, number, rows, amount, top, reach, slope):
    order = jax.random.permutation(key, amount)
    packed, common = portions_of(amount, rows * top, reach, slope, True), portions_of(amount, rows * top, reach, slope, False)
    places = jnp.arange(amount)

    def named(tallies, turn):
        used = int((tallies > 0).sum())
        fixed = max(1, used // 4)
        shifted = fixed + (places - fixed + turn * (used - fixed)) % max(1, amount - fixed)
        return jnp.zeros((amount,), jnp.int32).at[order[jnp.where(places < fixed, places, shifted)]].set(jnp.asarray(tallies, jnp.int32))

    tallies = jnp.where(number % 4 == 0, named(packed, number // 4), named(common, number - number // 4 - 1))
    mixed = jax.random.permutation(jax.random.fold_in(own, 3), amount)
    giver, sink = mixed[0:amount // 2 * 2:2], mixed[1:amount // 2 * 2:2]
    room = jnp.minimum(tallies[giver] - 1, reach - tallies[sink]) // 2
    room = jnp.where((giver == order[0]) | (sink == order[0]) | (tallies[sink] == 0), 0, jnp.maximum(room, 0))
    shifted = jax.random.randint(jax.random.fold_in(own, 4), (amount // 2,), 0, 1 << 20) % (room + 1)
    tallies = tallies.at[giver].add(-shifted).at[sink].add(shifted)
    items = jnp.searchsorted(jnp.cumsum(tallies), jnp.arange(rows * top), side="right").astype(jnp.int32)
    listing = items.reshape(top, rows).T
    listing = listing[jax.random.permutation(jax.random.fold_in(own, 1), rows)]
    turn = jax.random.randint(jax.random.fold_in(own, 2), (rows, 1), 0, top)
    return jnp.take_along_axis(listing, (jnp.arange(top)[None, :] + turn) % top, axis=1)


def portions_of(amount, total, most, slope, full):
    portions = [(1 << 20) // math.isqrt(standing ** slope) + 1 for standing in range(1, amount + 1)]
    largest = most if full else min(most, max(-(-total // amount), total * portions[0] // sum(portions)))
    least = 1 if total - largest >= amount - 1 else 0
    given, spare = [largest] + [least] * (amount - 1), total - largest - least * (amount - 1)
    while spare > 0:
        movable = [i for i in range(1, amount) if given[i] < largest] or [i for i in range(1, amount) if given[i] < most]
        mass, budget = sum([portions[i] for i in movable]), spare
        for i in movable:
            addition = min(most - given[i], max(1, budget * portions[i] // mass), spare)
            given[i] = given[i] + addition
            spare = spare - addition
    return np.array(given)


def centred(key, extent, spread, most, cuts=(), dtype=jnp.bfloat16):
    level = block_scale(key, extent, cuts, -0.22, 0.18) if cuts else 1.0
    array = jax.random.normal(key, extent, jnp.float32) * spread * level
    return jnp.minimum(jnp.maximum(array, -most), most).astype(dtype)


def setup_inputs(seed: int = 0) -> dict:
    key_of = jax.random.split(jax.random.key(seed), 12)
    atm_tangent = centred(key_of[0], (LA, ATM_CELLS), 1.0, 6.0, ((1, 128),), jnp.float32)
    atm_mixing = jnp.clip(0.049804688 + 0.18945312 * jax.random.uniform(key_of[1], (LA - 1, ATM_CELLS), jnp.float32) ** block_scale(key_of[1], (LA - 1, ATM_CELLS), ((1, 128),), -0.2, 0.2), 0.049804688, 0.23925781).astype(jnp.bfloat16)
    flux_coef = centred(key_of[2], (FLD, LA), LA ** -0.5, 0.75, (), jnp.float32)
    remap_weight = centred(key_of[3], (BLOCKS * KO, B, B), B ** -0.5, 0.5, ((0, 128),))
    target_device_keys = jax.random.split(jax.random.fold_in(key_of[4], 1), BLOCKS // NBA)
    target_device_turns = jax.random.permutation(jax.random.fold_in(key_of[4], 3), BLOCKS // NBA)
    target_device = jax.vmap(lambda own, number: deal_out(jax.random.fold_in(key_of[4], 2), own, number, NBA, DEVICES, KO, CAP, 2))(target_device_keys, target_device_turns).reshape((BLOCKS, KO))
    target_row = with_ends(jax.random.randint(key_of[5], (BLOCKS, KO), 0, OY), jax.random.fold_in(key_of[5], 1), 0, OY - 1).astype(jnp.int32)
    ocean_tangent = centred(key_of[6], (LO, NY, NX), 1.0, 6.0, ((1, 8), (2, 16)), jnp.float32)
    ocean_mixing = jnp.clip(jax.random.uniform(key_of[7], (LO - 1,), jnp.float32, 0.02, 0.2), 0.02, 0.2)
    penetration = centred(key_of[8], (LO, FLD), 0.12, 0.75, (), jnp.float32)
    sea_mask = with_ends((jax.random.randint(key_of[9], (NY, NX), 0, 4) < 3).astype(jnp.int32), jax.random.fold_in(key_of[9], 1), 0, 1)
    ocean_adjoint = centred(key_of[10], (LO, NY, NX), 1.0, 6.0, ((1, 8), (2, 16)), jnp.float32)
    return {"atm_tangent": atm_tangent, "atm_mixing": atm_mixing, "flux_coef": flux_coef, "remap_weight": remap_weight, "target_device": target_device, "target_row": target_row, "ocean_tangent": ocean_tangent, "ocean_mixing": ocean_mixing, "penetration": penetration, "sea_mask": sea_mask, "ocean_adjoint": ocean_adjoint}


horizontal_rate = 0.1


def column_mix(state, mixing):
    fluxes = mixing * (state[1:] - state[:-1])
    edge = jnp.zeros_like(state[:1])
    return state + jnp.concatenate([fluxes, edge], axis=0) - jnp.concatenate([edge, fluxes], axis=0)


def ocean_step(state, mixing):
    padded = jnp.pad(state, ((0, 0), (1, 1), (0, 0)))
    padded = jnp.concatenate([padded[:, :, -1:], padded, padded[:, :, :1]], axis=2)
    center = padded[:, 1:-1, 1:-1]
    laplace = padded[:, 2:, 1:-1] + padded[:, :-2, 1:-1] + padded[:, 1:-1, 2:] + padded[:, 1:-1, :-2] - 4.0 * center
    return column_mix(center, mixing[:, None, None]) + horizontal_rate * laplace


def reference(atm_tangent, atm_mixing, flux_coef, remap_weight, target_device, target_row, ocean_tangent, ocean_mixing, penetration, sea_mask, ocean_adjoint):
    highest = lax.Precision.HIGHEST
    mixing = atm_mixing.astype(jnp.float32)
    state = atm_tangent
    for sweep in range(ATM_SWEEPS):
        state = column_mix(state, mixing)
    surface_flux = jnp.dot(flux_coef, state, precision=highest)
    blocks = surface_flux.reshape(FLD, DEVICES, NBA, B).transpose(1, 2, 0, 3)
    weights = remap_weight.reshape(DEVICES, NBA, KO, B, B)

    def forward_one(pair):
        block_set, weight_set = pair
        out = jnp.einsum("afb,akbc->akfc", block_set, weight_set.astype(jnp.float32), precision=highest)
        return out.reshape(NBA * KO, FLD, B)

    contribution = lax.map(forward_one, (blocks, weights))
    target = (target_device * OY + target_row).reshape(-1).astype(jnp.int32)
    gathered = jax.ops.segment_sum(contribution.reshape(-1, FLD, B), target, DEVICES * OY)
    ocean_flux = gathered.reshape(N_FACE, N_TILE, OY, FLD, B).transpose(3, 0, 2, 1, 4).reshape(FLD, NY, NX)
    sea = sea_mask.astype(jnp.float32)
    forced = ocean_tangent + jnp.einsum("lf,fyx->lyx", penetration, ocean_flux, precision=highest)
    for sweep in range(OCEAN_STEPS):
        forced = ocean_step(forced, ocean_mixing)
    ocean_forward = forced * sea
    backward = ocean_adjoint * sea
    for sweep in range(OCEAN_STEPS):
        backward = ocean_step(backward, ocean_mixing)
    flux_adjoint = jnp.einsum("lf,lyx->fyx", penetration, backward, precision=highest)
    adjoint_blocks = flux_adjoint.reshape(FLD, N_FACE, OY, N_TILE, B).transpose(1, 3, 2, 0, 4).reshape(DEVICES * OY, FLD, B)
    returned = adjoint_blocks[target].reshape(DEVICES, NBA, KO, FLD, B)

    def backward_one(pair):
        piece, weight_set = pair
        return jnp.einsum("akfc,akbc->afb", piece, weight_set.astype(jnp.float32), precision=highest)

    block_adjoint = lax.map(backward_one, (returned, weights))
    block_adjoint = block_adjoint.transpose(2, 0, 1, 3).reshape(FLD, ATM_CELLS)
    adjoint_state = jnp.dot(flux_coef.T, block_adjoint, precision=highest)
    for sweep in range(ATM_SWEEPS):
        adjoint_state = column_mix(adjoint_state, mixing)
    return ocean_forward, backward, adjoint_state
```

```python
import functools

import jax
import jax.numpy as jnp
from jax import lax
from jax.experimental import pallas as pl
from jax.experimental.pallas import tpu as pltpu
from jax.sharding import PartitionSpec as P

ATM_SWEEPS = 4
HRATE = 0.1
LA = 64
LO = 75
FLD = 4
B = 128
NBA = 64
KO = 4
OY = 64
CAP = 4
DEV = 128
MSG = CAP * FLD + 1
GRP = 8
PLANES = 3
ROWS = 72
F32 = jnp.float32
BF16 = jnp.bfloat16
VMEM_LIMIT = 56 * 1024 * 1024


def split2(v):
    hi = v.astype(BF16)
    return hi, (v - hi.astype(F32)).astype(BF16)


def dot(a, b, dims=((1,), (0,))):
    return lax.dot_general(a, b, (dims, ((), ())), preferred_element_type=F32)


def lanes(rows):
    return lax.broadcasted_iota(jnp.int32, (rows, B), 1)


def sweeps(x, mix):
    for _ in range(ATM_SWEEPS):
        flow = mix * (pltpu.roll(x, LA - 1, 0) - x)
        x = x + flow - pltpu.roll(flow, 1, 0)
    return x


def mixing_of(mix_ref, i):
    rows = mix_ref[:, i * B : (i + 1) * B].astype(F32)
    return jnp.concatenate([rows, jnp.zeros((1, B), F32)], axis=0)


def atm_forward_kernel(td_ref, tr_ref, coef_ref, x_ref, mix_ref, w_ref, out_ref, slot_ref, count):
    step = pl.program_id(0)

    @pl.when(step == 0)
    def _():
        out_ref[...] = jnp.zeros_like(out_ref)

        def clear(d, c):
            count[d] = 0
            return c

        lax.fori_loop(0, DEV, clear, 0, unroll=8)

    ch, cl = split2(coef_ref[...])
    left = jnp.concatenate(
        [jnp.concatenate([ch, ch], axis=1), jnp.concatenate([cl, cl], axis=1)], axis=0
    )
    lane = lanes(1)
    for i in range(GRP):
        x = sweeps(x_ref[:, i * B : (i + 1) * B], mixing_of(mix_ref, i))
        xh, xl = split2(x)
        flux = dot(left, jnp.concatenate([xh, xl], axis=0))
        flux = flux[:FLD] + flux[FLD:]
        fh, fl = split2(flux)
        pair = jnp.concatenate([fh, fl], axis=0)
        for k in range(KO):
            moved = dot(pair, w_ref[i * KO + k])
            moved = moved[:FLD] + moved[FLD:]
            row = step * GRP + i
            dev = td_ref[row, k]
            place = count[dev]
            count[dev] = place + 1
            slot_ref[row * KO + k] = dev * CAP + place
            at = dev * MSG
            out_ref[pl.ds(at + place * FLD, FLD), :] = moved
            label = (tr_ref[row, k] + 1).astype(F32)
            old = out_ref[pl.ds(at + MSG - 1, 1), :]
            out_ref[pl.ds(at + MSG - 1, 1), :] = jnp.where(lane == place, label, old)


def atm_forward(td, tr, coef, x, mix, w):
    cols = GRP * B
    smem = pl.BlockSpec(memory_space=pltpu.SMEM)
    return pl.pallas_call(
        atm_forward_kernel,
        grid=(NBA // GRP,),
        in_specs=[
            smem,
            smem,
            pl.BlockSpec((FLD, LA), lambda s: (0, 0)),
            pl.BlockSpec((LA, cols), lambda s: (0, s)),
            pl.BlockSpec((LA - 1, cols), lambda s: (0, s)),
            pl.BlockSpec((GRP * KO, B, B), lambda s: (s, 0, 0)),
        ],
        out_specs=[pl.BlockSpec((DEV * MSG, B), lambda s: (0, 0)), smem],
        out_shape=[
            jax.ShapeDtypeStruct((DEV * MSG, B), F32),
            jax.ShapeDtypeStruct((NBA * KO,), jnp.int32),
        ],
        scratch_shapes=[pltpu.SMEM((DEV,), jnp.int32)],
        compiler_params=pltpu.CompilerParams(vmem_limit_bytes=VMEM_LIMIT),
        name="atm_forward",
    )(td, tr, coef, x, mix, w)


def atm_adjoint_kernel(slot_ref, coef_ref, back_ref, mix_ref, w_ref, out_ref):
    step = pl.program_id(0)
    ch, cl = split2(coef_ref[...].T)
    left = jnp.concatenate([ch, ch, cl, jnp.zeros_like(cl)], axis=1)
    for i in range(GRP):
        total = None
        for k in range(KO):
            slot = slot_ref[(step * GRP + i) * KO + k]
            ph, pll = split2(back_ref[slot])
            part = dot(jnp.concatenate([ph, pll], axis=0), w_ref[i * KO + k], ((1,), (1,)))
            total = part if total is None else total + part
        total = total[:FLD] + total[FLD:]
        bh, bl = split2(total)
        x = dot(left, jnp.concatenate([bh, bl, bh, jnp.zeros_like(bh)], axis=0))
        out_ref[:, i * B : (i + 1) * B] = sweeps(x, mixing_of(mix_ref, i))


def atm_adjoint(slots, coef, back, mix, w):
    cols = GRP * B
    return pl.pallas_call(
        atm_adjoint_kernel,
        grid=(NBA // GRP,),
        in_specs=[
            pl.BlockSpec(memory_space=pltpu.SMEM),
            pl.BlockSpec((FLD, LA), lambda s: (0, 0)),
            pl.BlockSpec((DEV * CAP, FLD, B), lambda s: (0, 0, 0)),
            pl.BlockSpec((LA - 1, cols), lambda s: (0, s)),
            pl.BlockSpec((GRP * KO, B, B), lambda s: (s, 0, 0)),
        ],
        out_specs=pl.BlockSpec((LA, cols), lambda s: (0, s)),
        out_shape=jax.ShapeDtypeStruct((LA, NBA * B), F32),
        compiler_params=pltpu.CompilerParams(vmem_limit_bytes=VMEM_LIMIT),
        name="atm_adjoint",
    )(slots, coef, back, mix, w)


def pack_kernel(x_ref, mask_ref, north_ref, south_ref, out_ref):
    sea = None if mask_ref is None else mask_ref[...].astype(F32)
    lane = lanes(1)
    out_ref[...] = jnp.zeros_like(out_ref)
    for plane in range(PLANES):
        held = jnp.zeros((OY, B), F32)
        rim = jnp.zeros((2, B), F32)
        for m in range(min(32, LO - 32 * plane)):
            level = 32 * plane + m
            x = x_ref[level]
            if sea is not None:
                x = x * sea
            mine = lane // 4 == m
            held = jnp.where(mine, pltpu.roll(x, (4 * m + 2) % B, 1), held)
            edge = jnp.concatenate([south_ref[level, 0:1], north_ref[level, 1:2]], axis=0)
            rim = jnp.where(mine, pltpu.roll(edge, (4 * m + 2) % B, 1), rim)
        out_ref[plane, 0:OY] = held
        out_ref[plane, OY : OY + 1] = rim[0:1]
        out_ref[plane, ROWS - 1 : ROWS] = rim[1:2]


def pack_columns(x, mask, north, south):
    out = jax.ShapeDtypeStruct((PLANES, ROWS, B), F32)
    params = pltpu.CompilerParams(vmem_limit_bytes=VMEM_LIMIT)
    if mask is None:
        kernel = lambda x_ref, n_ref, s_ref, o_ref: pack_kernel(x_ref, None, n_ref, s_ref, o_ref)
        return pl.pallas_call(kernel, out_shape=out, compiler_params=params, name="pack_forced")(
            x, north, south
        )
    return pl.pallas_call(pack_kernel, out_shape=out, compiler_params=params, name="pack_adjoint")(
        x, mask, north, south
    )


def ocean_kernel(adjoint, k_ref, ends_ref, pen_ref, x_ref, mask_ref, north_ref, south_ref,
                 own_ref, west_ref, east_ref, *rest):
    if adjoint:
        out_ref, flux_ref, state, first, first_cols = rest
    else:
        out_ref, state, first, first_cols = rest
    sea = mask_ref[...].astype(F32)
    open_north = ends_ref[0].astype(F32)
    open_south = ends_ref[1].astype(F32)

    state[:, OY:ROWS, :] = jnp.zeros((LO + 1, ROWS - OY, B), F32)
    state[0:LO, OY : OY + 2, :] = south_ref[...]
    state[0:LO, ROWS - 2 : ROWS, :] = north_ref[...]
    state[LO, 0:OY] = jnp.zeros((OY, B), F32)

    def fill(level, carry):
        v = x_ref[level]
        state[level, 0:OY] = v * sea if adjoint else v
        return carry

    lax.fori_loop(0, LO, fill, 0, unroll=3)

    lane = lanes(1)
    part = lane % 4
    ups, downs = [], []
    for plane in range(PLANES):
        up = jnp.zeros((1, B), F32)
        down = jnp.zeros((1, B), F32)
        for m in range(min(32, LO - 32 * plane)):
            level = 32 * plane + m
            mine = lane // 4 == m
            if level < LO - 1:
                up = jnp.where(mine, k_ref[level], up)
            if level > 0:
                down = jnp.where(mine, k_ref[level - 1], down)
        ups.append(up)
        downs.append(down)
    own = [own_ref[p] for p in range(PLANES)]
    outer = [jnp.where(part < 2, west_ref[p], east_ref[p]) for p in range(PLANES)]

    def swapped(v):
        return jnp.where(part == 2, pltpu.roll(v, 1, 1), pltpu.roll(v, B - 1, 1))

    first_cols[0] = jnp.zeros((PLANES, ROWS, B), F32)
    first_cols[1] = jnp.zeros((PLANES, ROWS, B), F32)
    for p in range(PLANES):
        c = outer[p]
        first_cols[0, p] = swapped(c)
        higher = pltpu.roll(c, B - 4, 1)
        if p + 1 < PLANES:
            higher = jnp.where(lane < B - 4, higher, pltpu.roll(outer[p + 1], B - 4, 1))
        lower = pltpu.roll(c, 4, 1)
        if p > 0:
            lower = jnp.where(lane >= 4, lower, pltpu.roll(outer[p - 1], 4, 1))
        from_west = jnp.where(part == 1, pltpu.roll(c, 1, 1), pltpu.roll(own[p], 1, 1))
        from_east = jnp.where(part == 1, pltpu.roll(own[p], B - 1, 1), pltpu.roll(c, B - 1, 1))
        around = from_west + from_east + pltpu.roll(c, 1, 0) + pltpu.roll(c, ROWS - 1, 0)
        mixed = c + ups[p] * (higher - c) - downs[p] * (c - lower)
        first_cols[1, p] = swapped(mixed + HRATE * (around - 4.0 * c))

    ring = lax.broadcasted_iota(jnp.int32, (ROWS, B), 0)
    keep = jnp.where(ring == ROWS - 1, open_north, jnp.where(ring == OY, open_south, 1.0))
    wide = lanes(ROWS)
    lane_low, lane_high = wide == 0, wide == B - 1

    def beside(v, cols, level, low, high):
        edge = pltpu.roll(cols, B - 2 - 4 * (level % 32), 1)
        return jnp.where(low, edge, pltpu.roll(v, 1, 1)) + jnp.where(
            high, edge, pltpu.roll(v, B - 1, 1)
        )

    first[LO] = jnp.zeros((ROWS, B), F32)

    def one(level, flow_below):
        v = state[level]
        k = jnp.where(level < LO - 1, k_ref[jnp.minimum(level, LO - 2)], 0.0)
        flow = k * (state[level + 1] - v)
        around = (
            beside(v, first_cols[0, level // 32], level, lane_low, lane_high)
            + pltpu.roll(v, 1, 0)
            + pltpu.roll(v, ROWS - 1, 0)
        )
        first[level] = keep * (v + flow - flow_below + HRATE * (around - 4.0 * v))
        return flow

    lax.fori_loop(0, LO, one, jnp.zeros((ROWS, B), F32))

    def two(level, flow_below):
        full = first[level]
        v = full[0:OY]
        k = jnp.where(level < LO - 1, k_ref[jnp.minimum(level, LO - 2)], 0.0)
        flow = k * (first[level + 1, 0:OY] - v)
        around = (
            beside(v, first_cols[1, level // 32, 0:OY], level, lane_low[0:OY], lane_high[0:OY])
            + pltpu.roll(full, 1, 0)[0:OY]
            + pltpu.roll(full, ROWS - 1, 0)[0:OY]
        )
        done = v + flow - flow_below + HRATE * (around - 4.0 * v)
        out_ref[level] = done if adjoint else done * sea
        return flow

    lax.fori_loop(0, LO, two, jnp.zeros((OY, B), F32))

    if adjoint:
        for r in range(OY // 8):
            rows = pl.ds(8 * r, 8)

            def project(level, sums):
                v = out_ref[level, rows, :]
                return tuple(s + pen_ref[level, f] * v for f, s in enumerate(sums))

            sums = lax.fori_loop(
                0, LO, project, tuple(jnp.zeros((8, B), F32) for _ in range(FLD)), unroll=5
            )
            for f in range(FLD):
                flux_ref[rows, f * B : (f + 1) * B] = sums[f]


def ocean_steps(adjoint, k, ends, pen, x, mask, north, south, own, west, east):
    smem = pl.BlockSpec(memory_space=pltpu.SMEM)
    vmem = pl.BlockSpec(memory_space=pltpu.VMEM)
    shapes = [jax.ShapeDtypeStruct((LO, OY, B), F32)]
    if adjoint:
        shapes.append(jax.ShapeDtypeStruct((OY, FLD * B), F32))
    return pl.pallas_call(
        functools.partial(ocean_kernel, adjoint),
        in_specs=[smem, smem, smem] + [vmem] * 7,
        out_specs=[vmem] * len(shapes),
        out_shape=shapes,
        scratch_shapes=[
            pltpu.VMEM((LO + 1, ROWS, B), F32),
            pltpu.VMEM((LO + 1, ROWS, B), F32),
            pltpu.VMEM((2, PLANES, ROWS, B), F32),
        ],
        compiler_params=pltpu.CompilerParams(vmem_limit_bytes=VMEM_LIMIT),
        name="ocean_adjoint" if adjoint else "ocean_forward",
    )(k, ends, pen, x, mask, north, south, own, west, east)


def answer_kernel(msg_ref, flux_ref, out_ref):
    labels = msg_ref[pl.ds(MSG - 1, DEV, stride=MSG), :]
    gh, gl = split2(flux_ref[...])
    table = jnp.concatenate([gh, gl], axis=0)
    want = lax.broadcasted_iota(jnp.int32, (DEV, B), 1) % OY + 1
    for c in range(CAP):
        pick = (labels[:, c : c + 1].astype(jnp.int32) == want).astype(F32).astype(BF16)
        rows = dot(pick, table)
        for f in range(FLD):
            out_ref[pl.ds(c * FLD + f, DEV, stride=CAP * FLD), :] = rows[:, f * B : (f + 1) * B]


def answer(msg, flux):
    return pl.pallas_call(
        answer_kernel,
        out_shape=jax.ShapeDtypeStruct((DEV * CAP * FLD, B), F32),
        compiler_params=pltpu.CompilerParams(vmem_limit_bytes=VMEM_LIMIT),
        name="answer",
    )(msg, flux)


def force_kernel(pen_ref, msg_ref, x_ref, out_ref, north_ref, south_ref, flux):
    labels = msg_ref[pl.ds(MSG - 1, DEV, stride=MSG), :].T.astype(jnp.int32)
    rows = lax.broadcasted_iota(jnp.int32, (OY, DEV), 0) + 1
    total = jnp.zeros((OY, FLD * B), F32)
    for c in range(CAP):
        pick = (labels[c : c + 1, :] == rows).astype(F32).astype(BF16)
        data = jnp.concatenate(
            [msg_ref[pl.ds(c * FLD + f, DEV, stride=MSG), :] for f in range(FLD)], axis=1
        )
        dh, dl = split2(data)
        total = total + dot(pick, dh) + dot(pick, dl)
    flux[...] = total
    for r in range(OY // 8):
        rows = pl.ds(8 * r, 8)
        parts = [flux[rows, f * B : (f + 1) * B] for f in range(FLD)]

        def one(level, carry):
            v = x_ref[level, rows, :]
            for f in range(FLD):
                v = v + pen_ref[level, f] * parts[f]
            out_ref[level, rows, :] = v
            return carry

        lax.fori_loop(0, LO, one, 0, unroll=5)
    north_ref[...] = out_ref[:, 0:2, :]
    south_ref[...] = out_ref[:, OY - 2 : OY, :]


def force(pen, msg, x):
    smem = pl.BlockSpec(memory_space=pltpu.SMEM)
    vmem = pl.BlockSpec(memory_space=pltpu.VMEM)
    return pl.pallas_call(
        force_kernel,
        in_specs=[smem, vmem, vmem],
        out_specs=[vmem] * 3,
        out_shape=[
            jax.ShapeDtypeStruct((LO, OY, B), F32),
            jax.ShapeDtypeStruct((LO, 2, B), F32),
            jax.ShapeDtypeStruct((LO, 2, B), F32),
        ],
        scratch_shapes=[pltpu.VMEM((OY, FLD * B), F32)],
        compiler_params=pltpu.CompilerParams(vmem_limit_bytes=VMEM_LIMIT),
        name="force",
    )(pen, msg, x)


def swap_rows(low_rows, high_rows):
    count = lax.axis_size("face")
    south_going = [(i, i + 1) for i in range(count - 1)]
    north_going = [(i + 1, i) for i in range(count - 1)]
    north = lax.ppermute(high_rows, "face", south_going)
    south = lax.ppermute(low_rows, "face", north_going)
    return north, south


def swap_columns(packed):
    count = lax.axis_size("tile")
    east_going = [(i, (i + 1) % count) for i in range(count)]
    west_going = [((i + 1) % count, i) for i in range(count)]
    west = lax.ppermute(packed, "tile", east_going)
    east = lax.ppermute(packed, "tile", west_going)
    return west, east


def exchange(rows):
    return lax.all_to_all(rows, ("face", "tile"), split_axis=0, concat_axis=0, tiled=True)


def local(
    atm_tangent,
    atm_mixing,
    flux_coef,
    remap_weight,
    target_device,
    target_row,
    ocean_tangent,
    ocean_mixing,
    penetration,
    sea_mask,
    ocean_adjoint,
):
    face = lax.axis_index("face")
    ends = jnp.stack([face > 0, face < lax.axis_size("face") - 1]).astype(jnp.int32)
    sea = sea_mask.astype(F32)
    north, south = swap_rows(
        ocean_adjoint[:, 0:2] * sea[0:2], ocean_adjoint[:, OY - 2 : OY] * sea[OY - 2 : OY]
    )
    sent, slots = atm_forward(
        target_device, target_row, flux_coef, atm_tangent, atm_mixing, remap_weight
    )
    own = pack_columns(ocean_adjoint, sea_mask, north, south)
    west, east = swap_columns(own)
    arrived = exchange(sent.reshape(DEV, 1, MSG * B)).reshape(DEV * MSG, B)
    ocean_backward, flux_adjoint = ocean_steps(
        True, ocean_mixing, ends, penetration, ocean_adjoint, sea_mask, north, south, own, west, east
    )
    returned = exchange(answer(arrived, flux_adjoint).reshape(DEV, CAP, FLD, B))
    forced, low, high = force(penetration, arrived, ocean_tangent)
    north, south = swap_rows(low, high)
    own = pack_columns(forced, None, north, south)
    west, east = swap_columns(own)
    (ocean_forward,) = ocean_steps(
        False, ocean_mixing, ends, penetration, forced, sea_mask, north, south, own, west, east
    )
    atm = atm_adjoint(
        slots, flux_coef, returned.reshape(DEV * CAP, FLD, B), atm_mixing, remap_weight
    )
    return ocean_forward, ocean_backward, atm


def solution(mesh):
    placed = (
        P(None, ("face", "tile")),
        P(None, ("face", "tile")),
        P(),
        P(("face", "tile"), None, None),
        P(("face", "tile"), None),
        P(("face", "tile"), None),
        P(None, "face", "tile"),
        P(),
        P(),
        P("face", "tile"),
        P(None, "face", "tile"),
    )
    return jax.shard_map(
        local,
        mesh=mesh,
        in_specs=placed,
        out_specs=(P(None, "face", "tile"), P(None, "face", "tile"), P(None, ("face", "tile"))),
        check_vma=False,
    )
```

```python
import functools

import jax
import jax.numpy as jnp
from jax import lax
from jax.experimental import pallas as pl
from jax.experimental.pallas import tpu as pltpu
from jax.sharding import PartitionSpec as P

ATM_SWEEPS = 4
HRATE = 0.1
LA = 64
LO = 75
FLD = 4
B = 128
NBA = 64
KO = 4
OY = 64
CAP = 4
DEV = 128
MSG = CAP * FLD + 1
GRP = 8
STEPS = NBA // GRP
PLANES = 3
ROWS = 72
TOP = 16
TALL = 96
LEVELS = 25
F32 = jnp.float32
BF16 = jnp.bfloat16
MIB = 1024 * 1024
SMEM = pl.BlockSpec(memory_space=pltpu.SMEM)
VMEM = pl.BlockSpec(memory_space=pltpu.VMEM)
ANY = pl.BlockSpec(memory_space=pl.ANY)
PITCH = LA + 1
ALONE = 58


def params(mib):
    return pltpu.CompilerParams(vmem_limit_bytes=mib * MIB)


def f32(*shape):
    return jax.ShapeDtypeStruct(shape, F32)


def split2(v):
    hi = v.astype(BF16)
    return hi, (v - hi.astype(F32)).astype(BF16)


def dot(a, b, dims=((1,), (0,))):
    return lax.dot_general(a, b, (dims, ((), ())), preferred_element_type=F32)


def lanes(rows):
    return lax.broadcasted_iota(jnp.int32, (rows, B), 1)


def sweep_levels(load, mixing, emit):
    values = [{} for _ in range(ATM_SWEEPS + 1)]
    flows = [{} for _ in range(ATM_SWEEPS)]
    mix = {}
    for t in range(LA + ATM_SWEEPS):
        if t < LA:
            values[0][t] = load(t)
            if t < LA - 1:
                mix[t] = mixing(t)
        for s in range(ATM_SWEEPS):
            l = t - 1 - s
            if not 0 <= l < LA:
                continue
            v = values[s][l]
            done = v
            if l < LA - 1:
                flows[s][l] = mix[l] * (values[s][l + 1] - v)
                done = done + flows[s][l]
            if l > 0:
                done = done - flows[s][l - 1]
            values[s + 1][l] = done
            if s == ATM_SWEEPS - 1:
                emit(l, done)


def level_rows(ref, level):
    return ref[pl.ds(level, GRP, stride=PITCH), :]


def block_lanes(block):
    return pl.ds(pl.multiple_of(block * B, B), B)


def square(w_ref, block, k):
    at = block * KO + k
    return jnp.concatenate(
        [
            jnp.concatenate([w_ref[at], w_ref[at + 1]], axis=1),
            jnp.concatenate([w_ref[at + KO], w_ref[at + KO + 1]], axis=1),
        ],
        axis=0,
    )


def surface_flux_kernel(coef_ref, x_ref, mix_ref, out_ref, xs, ms):
    def work(step, carry):
        for b in range(GRP):
            at = block_lanes(step * GRP + b)
            xs[step % 2, pl.ds(b * PITCH, LA), :] = x_ref[:, at]
            ms[step % 2, pl.ds(b * PITCH, LA - 1), :] = mix_ref[:, at].astype(F32)
        sums = [None] * FLD

        def emit(level, v):
            for f in range(FLD):
                term = coef_ref[f, level] * v
                sums[f] = term if sums[f] is None else sums[f] + term

        sweep_levels(
            lambda l: level_rows(xs.at[step % 2], l), lambda l: level_rows(ms.at[step % 2], l), emit
        )
        for f in range(FLD):
            high = sums[f].astype(BF16).astype(F32)
            at = step * GRP * 2 * FLD + f
            out_ref[pl.ds(at, GRP, stride=2 * FLD), :] = high
            out_ref[pl.ds(at + FLD, GRP, stride=2 * FLD), :] = sums[f] - high
        return carry

    lax.fori_loop(0, STEPS, work, 0, unroll=2)


def surface_flux(coef, x, mix):
    return pl.pallas_call(
        surface_flux_kernel,
        in_specs=[SMEM, VMEM, VMEM],
        out_specs=VMEM,
        out_shape=f32(NBA * 2 * FLD, B),
        scratch_shapes=[pltpu.VMEM((2, GRP * PITCH, B), F32), pltpu.VMEM((2, GRP * PITCH, B), F32)],
        compiler_params=params(12),
        name="surface_flux",
    )(coef, x, mix)


def remap_kernel(td_ref, tr_ref, pair_ref, w_ref, out_ref, slot_ref, count):
    out_ref[...] = jnp.zeros_like(out_ref)

    def clear(d, c):
        count[d] = 0
        return c

    lax.fori_loop(0, DEV, clear, 0, unroll=8)
    lane = lanes(1)
    upper = lax.broadcasted_iota(jnp.int32, (4 * FLD, B), 0) < 2 * FLD

    def work(step, carry):
        for i in range(0, GRP, 2):
            row = step * GRP + i
            both = pair_ref[pl.ds(pl.multiple_of(row * 2 * FLD, 4 * FLD), 4 * FLD), :]
            lhs = jnp.concatenate(
                [jnp.where(upper, both, 0.0), jnp.where(upper, 0.0, both)], axis=1
            ).astype(BF16)
            for k in range(0, KO, 2):
                moved = dot(lhs, square(w_ref, row, k))
                for a in range(2):
                    total = moved[8 * a : 8 * a + 4] + moved[8 * a + 4 : 8 * a + 8]
                    for b in range(2):
                        dev = td_ref[k + b, row + a]
                        place = count[dev]
                        count[dev] = place + 1
                        slot_ref[(row + a) * KO + k + b] = dev * CAP + place
                        at = dev * MSG
                        out_ref[pl.ds(at + place * FLD, FLD), :] = total[:, b * B : (b + 1) * B]
                        label = (tr_ref[k + b, row + a] + 1).astype(F32)
                        last = pl.ds(at + MSG - 1, 1)
                        out_ref[last, :] = jnp.where(lane == place, label, out_ref[last, :])
        return carry

    lax.fori_loop(0, STEPS, work, 0, unroll=STEPS)


def remap(td, tr, pair, w):
    return pl.pallas_call(
        remap_kernel,
        in_specs=[SMEM, SMEM, VMEM, VMEM],
        out_specs=[VMEM, SMEM],
        out_shape=[f32(DEV * MSG, B), jax.ShapeDtypeStruct((NBA * KO,), jnp.int32)],
        scratch_shapes=[pltpu.SMEM((DEV,), jnp.int32)],
        compiler_params=params(16),
        name="remap",
    )(td, tr, pair, w)


def atm_adjoint_kernel(
    slot_ref, coef_ref, back_ref, mix_ref, w_hbm, out_hbm, w_ref, ms, total_ref, steps_ref, out_ref, sems
):
    cols = GRP * B

    def w_copy(s):
        part = pl.ds(s * GRP * KO, GRP * KO)
        return pltpu.make_async_copy(w_hbm.at[part], w_ref.at[part], sems.at[0, s])

    def out_copy(s):
        part = pl.ds(pl.multiple_of(s * cols, cols), cols)
        return pltpu.make_async_copy(out_ref.at[:, part], out_hbm.at[:, part], sems.at[1, s])

    for s in range(STEPS):
        w_copy(s).start()

    def work(step, carry):
        w_copy(step).wait()
        for i in range(0, GRP, 2):
            row = step * GRP + i
            total = None
            for k in range(0, KO, 2):
                blocks = []
                for a in range(2):
                    pieces = []
                    for b in range(2):
                        v = back_ref[slot_ref[(row + a) * KO + k + b]]
                        high = v.astype(BF16).astype(F32)
                        pieces.append(jnp.concatenate([high, v - high], axis=0))
                    blocks.append(jnp.concatenate(pieces, axis=1))
                lhs = jnp.concatenate(blocks, axis=0).astype(BF16)
                part = dot(lhs, square(w_ref, row, k), ((1,), (1,)))
                total = part if total is None else total + part
            total_ref[pl.ds(i * FLD, FLD), :] = total[0:4, 0:B] + total[4:8, 0:B]
            total_ref[pl.ds((i + 1) * FLD, FLD), :] = total[8:12, B:] + total[12:16, B:]
        for b in range(GRP):
            ms[pl.ds(b * PITCH, LA - 1), :] = mix_ref[:, block_lanes(step * GRP + b)].astype(F32)
        fields = [total_ref[pl.ds(f, GRP, stride=FLD), :] for f in range(FLD)]

        def load(level):
            v = coef_ref[0, level] * fields[0]
            for f in range(1, FLD):
                v = v + coef_ref[f, level] * fields[f]
            return v

        def emit(level, v):
            steps_ref[pl.ds(level, GRP, stride=PITCH), :] = v

        sweep_levels(load, lambda l: level_rows(ms, l), emit)
        for b in range(GRP):
            out_ref[:, block_lanes(step * GRP + b)] = steps_ref[pl.ds(b * PITCH, LA), :]
        out_copy(step).start()
        return carry

    lax.fori_loop(0, STEPS, work, 0, unroll=2)
    for s in range(STEPS):
        out_copy(s).wait()


def atm_adjoint(slots, coef, back, mix, w):
    return pl.pallas_call(
        atm_adjoint_kernel,
        in_specs=[SMEM, SMEM, VMEM, VMEM, ANY],
        out_specs=ANY,
        out_shape=f32(LA, NBA * B),
        scratch_shapes=[
            pltpu.VMEM((NBA * KO, B, B), BF16),
            pltpu.VMEM((GRP * PITCH, B), F32),
            pltpu.VMEM((GRP * FLD, B), F32),
            pltpu.VMEM((GRP * PITCH, B), F32),
            pltpu.VMEM((LA, NBA * B), F32),
            pltpu.SemaphoreType.DMA((2, STEPS)),
        ],
        compiler_params=params(ALONE),
        name="atm_adjoint",
    )(slots, coef, back, mix, w)


def rows_kernel(a_hbm, t_hbm, m_hbm, low_ref, high_ref, a_ref, t_ref, m_ref, sems):
    copies = []
    for i, r in enumerate((0, OY - 8)):
        rows = pl.ds(r, 8)
        copies += [
            pltpu.make_async_copy(a_hbm.at[:, rows], a_ref.at[i], sems.at[0, i]),
            pltpu.make_async_copy(t_hbm.at[:, rows], t_ref.at[i], sems.at[1, i]),
            pltpu.make_async_copy(m_hbm.at[rows], m_ref.at[i], sems.at[2, i]),
        ]
    for c in copies:
        c.start()
    for c in copies:
        c.wait()
    low_ref[0:LO] = a_ref[0, :, 0:2, :] * m_ref[0, 0:2].astype(F32)
    low_ref[LO:] = t_ref[0, :, 0:2, :]
    high_ref[0:LO] = a_ref[1, :, 6:8, :] * m_ref[1, 6:8].astype(F32)
    high_ref[LO:] = t_ref[1, :, 6:8, :]


def edge_rows(adjoint, tangent, mask):
    return pl.pallas_call(
        rows_kernel,
        in_specs=[ANY] * 3,
        out_specs=[VMEM, VMEM],
        out_shape=[f32(2 * LO, 2, B), f32(2 * LO, 2, B)],
        scratch_shapes=[
            pltpu.VMEM((2, LO, 8, B), F32),
            pltpu.VMEM((2, LO, 8, B), F32),
            pltpu.VMEM((2, 8, B), jnp.int32),
            pltpu.SemaphoreType.DMA((3, 2)),
        ],
        compiler_params=params(ALONE),
        name="edge_rows",
    )(adjoint, tangent, mask)


def level_lanes(plane):
    return range(min(32, LO - 32 * plane))


def pack_kernel(a_ref, t_ref, mask_ref, north_ref, south_ref, own_ref, east_ref, west_ref):
    sea = mask_ref[...].astype(F32)
    lane = lanes(1)
    part = lane % 4
    for plane in range(PLANES):
        held = []
        for at, x_ref in ((0, a_ref), (LO, t_ref)):
            body = jnp.zeros((OY, B), F32)
            rim = jnp.zeros((2, B), F32)
            for m in level_lanes(plane):
                level = 32 * plane + m
                mine = lane // 4 == m
                body = jnp.where(mine, pltpu.roll(x_ref[level], (4 * m + 2) % B, 1), body)
                edge = jnp.concatenate(
                    [south_ref[at + level, 0:1], north_ref[at + level, 1:2]], axis=0
                )
                rim = jnp.where(mine, pltpu.roll(edge, (4 * m + 2) % B, 1), rim)
            if at == 0:
                body = body * jnp.where(part < 2, edge_mask(sea, part, True), edge_mask(sea, part, False))
            held.append(
                jnp.concatenate([body, rim[0:1], jnp.zeros((6, B), F32), rim[1:2]], axis=0)
            )
        adj, tan = held
        own_ref[0, plane] = adj
        own_ref[1, plane] = tan
        east_ref[plane] = jnp.where(part < 2, adj, pltpu.roll(tan, 2, 1))
        west_ref[plane] = jnp.where(part < 2, pltpu.roll(adj, B - 2, 1), tan)


def edge_mask(sea, part, high):
    first = B - 2 if high else 0
    return jnp.where(part % 2 == 0, sea[:, first : first + 1], sea[:, first + 1 : first + 2])


def pack_columns(adjoint, tangent, mask, north, south):
    return pl.pallas_call(
        pack_kernel,
        out_shape=[f32(2, PLANES, ROWS, B), f32(PLANES, ROWS, B), f32(PLANES, ROWS, B)],
        compiler_params=params(12),
        name="pack_columns",
    )(adjoint, tangent, mask, north, south)


def lateral_table():
    r = lax.broadcasted_iota(jnp.int32, (B, B), 0)
    c = lax.broadcasted_iota(jnp.int32, (B, B), 1)
    near = ((r - c == 1) | (c - r == 1)).astype(F32).astype(BF16)
    return jnp.concatenate([near, near], axis=0)


def swapped(v, part):
    return jnp.where(part == 2, pltpu.roll(v, 1, 1), pltpu.roll(v, B - 1, 1))


def around_rows(v):
    return pltpu.roll(v, 1, 0) + pltpu.roll(v, ROWS - 1, 0)


def ocean_kernel(adjoint, k_ref, ends_ref, pen_ref, x_ref, mask_ref, north_ref, south_ref,
                 own_ref, west_ref, east_ref, *rest):
    if adjoint:
        out_hbm, flux_ref, state, first, fix, out_ref, sem = rest
    else:
        out_hbm, state, first, fix, out_ref, sem = rest
    sea = mask_ref[...].astype(F32)

    state[:, 8:TOP, :] = jnp.zeros((LO + 1, 8, B), F32)
    state[:, TOP + OY : TOP + OY + 8, :] = jnp.zeros((LO + 1, 8, B), F32)
    state[0:LO, TOP - 2 : TOP, :] = north_ref[...]
    state[0:LO, TOP + OY : TOP + OY + 2, :] = south_ref[...]
    state[LO, TOP : TOP + OY] = jnp.zeros((OY, B), F32)

    def fill(level, carry):
        v = x_ref[level]
        state[level, TOP : TOP + OY] = v * sea if adjoint else v
        return carry

    lax.fori_loop(0, LO, fill, 0, unroll=5)

    lane = lanes(1)
    part = lane % 4
    ups, downs = [], []
    for plane in range(PLANES):
        up = jnp.zeros((1, B), F32)
        down = jnp.zeros((1, B), F32)
        for m in level_lanes(plane):
            level = 32 * plane + m
            mine = lane // 4 == m
            if level < LO - 1:
                up = jnp.where(mine, k_ref[level], up)
            if level > 0:
                down = jnp.where(mine, k_ref[level - 1], down)
        ups.append(up)
        downs.append(down)
    own = [own_ref[0, p] for p in range(PLANES)]
    if adjoint:
        outer = [
            jnp.where(part < 2, west_ref[p], pltpu.roll(east_ref[p], 2, 1)) for p in range(PLANES)
        ]
    else:
        outer = [
            jnp.where(part < 2, pltpu.roll(west_ref[p], B - 2, 1), east_ref[p])
            for p in range(PLANES)
        ]

    def vertical(vs, p):
        c = vs[p]
        higher = pltpu.roll(c, B - 4, 1)
        if p + 1 < PLANES:
            higher = jnp.where(lane < B - 4, higher, pltpu.roll(vs[p + 1], B - 4, 1))
        lower = pltpu.roll(c, 4, 1)
        if p > 0:
            lower = jnp.where(lane >= 4, lower, pltpu.roll(vs[p - 1], 4, 1))
        return c + ups[p] * (higher - c) - downs[p] * (c - lower)

    inner = (part == 1) | (part == 2)
    added = [jnp.where(inner, HRATE * swapped(c, part), 0.0) for c in outer]
    for p in range(PLANES):
        c = outer[p]
        from_west = jnp.where(part == 1, pltpu.roll(c, 1, 1), pltpu.roll(own[p], 1, 1))
        from_east = jnp.where(part == 1, pltpu.roll(own[p], B - 1, 1), pltpu.roll(c, B - 1, 1))
        beyond = vertical(outer, p) + HRATE * (from_west + from_east + around_rows(c) - 4.0 * c)
        e = added[p]
        side = HRATE * (pltpu.roll(e, B - 1, 1) + pltpu.roll(e, 1, 1))
        here = vertical(added, p) + HRATE * (around_rows(e) - 4.0 * e + swapped(beyond, part))
        fix[p] = jnp.where(inner, here, side)[0:OY]

    table = lateral_table()
    first[LO] = jnp.zeros((TALL, B), F32)
    row = lax.broadcasted_iota(jnp.int32, (OY + 16, B), 0) + 8
    keep = jnp.where(
        row == TOP - 1, ends_ref[0].astype(F32), jnp.where(row == TOP + OY, ends_ref[1].astype(F32), 1.0)
    )
    wide = lanes(OY)
    edge_lane = (wide < 2) | (wide >= B - 2)

    def step(src, start, count, second):
        rows = pl.ds(start, count)

        def body(group, below):
            base = group * LEVELS
            vs = [src[base + j, rows, :] for j in range(LEVELS + 1)]
            hi, lo = split2(jnp.concatenate(vs[:LEVELS], axis=0))
            side = dot(jnp.concatenate([hi, lo], axis=1), table)
            for j in range(LEVELS):
                level = base + j
                v = vs[j]
                k = jnp.where(level < LO - 1, k_ref[jnp.minimum(level, LO - 2)], 0.0)
                flow = k * (vs[j + 1] - v)
                near = (
                    src[level, pl.ds(start - 1, count), :]
                    + src[level, pl.ds(start + 1, count), :]
                    + side[j * count : (j + 1) * count]
                )
                done = v * (1.0 - 4.0 * HRATE) + (flow - below) + HRATE * near
                if second:
                    shift = (2 * B - 2 - 4 * (level % 32)) % B
                    extra = pltpu.roll(fix[level // 32], shift, 1)
                    done = done + jnp.where(edge_lane, extra, 0.0)
                    out_ref[level] = done
                else:
                    first[level, rows, :] = done * keep
                below = flow
            return below

        lax.fori_loop(0, LO // LEVELS, body, jnp.zeros((count, B), F32))

    step(state, 8, OY + 16, False)
    step(first, TOP, OY, True)
    out_copy = pltpu.make_async_copy(out_ref, out_hbm, sem.at[0])
    out_copy.start()

    if adjoint:
        tall = 32
        for r in range(0, OY, tall):
            rows = pl.ds(r, tall)

            def project(level, sums):
                v = out_ref[level, rows, :]
                return tuple(s + pen_ref[f, level] * v for f, s in enumerate(sums))

            sums = lax.fori_loop(
                0, LO, project, tuple(jnp.zeros((tall, B), F32) for _ in range(FLD)), unroll=5
            )
            for f in range(FLD):
                flux_ref[rows, f * B : (f + 1) * B] = sums[f]
    out_copy.wait()


def ocean_steps(adjoint, k, ends, pen, x, mask, north, south, own, west, east):
    at = 0 if adjoint else 1
    rim = pl.BlockSpec((LO, 2, B), lambda i: (at, 0, 0))
    full = lambda *shape: pl.BlockSpec(shape, lambda i: (0,) * len(shape))
    shapes = [f32(LO, OY, B)]
    outs = [ANY]
    if adjoint:
        shapes.append(f32(OY, FLD * B))
        outs.append(full(OY, FLD * B))
    return pl.pallas_call(
        functools.partial(ocean_kernel, adjoint),
        grid=(1,),
        in_specs=[
            SMEM,
            SMEM,
            SMEM,
            full(LO, OY, B),
            full(OY, B),
            rim,
            rim,
            pl.BlockSpec((1, PLANES, ROWS, B), lambda i: (at, 0, 0, 0)),
            full(PLANES, ROWS, B),
            full(PLANES, ROWS, B),
        ],
        out_specs=outs,
        out_shape=shapes,
        scratch_shapes=[
            pltpu.VMEM((LO + 1, TALL, B), F32),
            pltpu.VMEM((LO + 1, TALL, B), F32),
            pltpu.VMEM((PLANES, OY, B), F32),
            pltpu.VMEM((LO, OY, B), F32),
            pltpu.SemaphoreType.DMA((1,)),
        ],
        compiler_params=params(24),
        name="ocean_adjoint" if adjoint else "ocean_tangent",
    )(k, ends, pen, x, mask, north, south, own, west, east)


def answer_kernel(msg_ref, flux_ref, out_ref):
    labels = msg_ref[pl.ds(MSG - 1, DEV, stride=MSG), :]
    gh, gl = split2(flux_ref[...])
    table = jnp.concatenate([gh, gl], axis=0)
    want = lax.broadcasted_iota(jnp.int32, (DEV, B), 1) % OY + 1
    for c in range(CAP):
        pick = (labels[:, c : c + 1].astype(jnp.int32) == want).astype(F32).astype(BF16)
        rows = dot(pick, table)
        for f in range(FLD):
            out_ref[pl.ds(c * FLD + f, DEV, stride=CAP * FLD), :] = rows[:, f * B : (f + 1) * B]


def answer(msg, flux):
    return pl.pallas_call(
        answer_kernel,
        out_shape=f32(DEV * CAP * FLD, B),
        compiler_params=params(12),
        name="answer",
    )(msg, flux)


def collect_kernel(msg_ref, flux_ref, low_ref, high_ref):
    labels = msg_ref[pl.ds(MSG - 1, DEV, stride=MSG), :].T.astype(jnp.int32)
    rows = lax.broadcasted_iota(jnp.int32, (OY, DEV), 0) + 1
    total = jnp.zeros((OY, FLD * B), F32)
    for c in range(CAP):
        pick = (labels[c : c + 1, :] == rows).astype(F32).astype(BF16)
        data = jnp.concatenate(
            [msg_ref[pl.ds(c * FLD + f, DEV, stride=MSG), :] for f in range(FLD)], axis=1
        )
        dh, dl = split2(data)
        total = total + dot(jnp.concatenate([pick, pick], axis=1), jnp.concatenate([dh, dl], axis=0))
    for f in range(FLD):
        v = total[:, f * B : (f + 1) * B]
        flux_ref[f] = v
        low_ref[f] = v[0:2]
        high_ref[f] = v[OY - 2 : OY]


def collect(msg):
    return pl.pallas_call(
        collect_kernel,
        out_shape=[f32(FLD, OY, B), f32(FLD, 2, B), f32(FLD, 2, B)],
        compiler_params=params(12),
        name="collect",
    )(msg)


def circular(flux_ref, north_ref, south_ref, f):
    return jnp.concatenate(
        [flux_ref[f], south_ref[f], jnp.zeros((ROWS - OY - 4, B), F32), north_ref[f]], axis=0
    )


def flux_columns_kernel(flux_ref, north_ref, south_ref, own_ref, out_ref):
    lane = lanes(1)
    held = jnp.zeros((ROWS, B), F32)
    for f in range(FLD):
        v = circular(flux_ref, north_ref, south_ref, f)
        held = jnp.where(lane // 4 == f, pltpu.roll(v, 4 * f + 2, 1), held)
    own_ref[...] = held
    square = jnp.concatenate([held, jnp.zeros((B - ROWS, B), F32)], axis=0)
    out_ref[...] = square.T[0 : 4 * FLD]


def flux_columns(flux, north, south):
    return pl.pallas_call(
        flux_columns_kernel,
        out_shape=[f32(ROWS, B), f32(4 * FLD, B)],
        compiler_params=params(12),
        name="flux_columns",
    )(flux, north, south)


def unsent(ref):
    return jnp.concatenate([ref[...], jnp.zeros((B - 4 * FLD, B), F32)], axis=0).T[0:ROWS]


def apply_flux_kernel(
    coef_ref, ends_ref, x_ref, mask_ref, flux_ref, north_ref, south_ref, own_ref, west_ref, east_ref,
    out_hbm, terms, out_ref, sems
):
    lane = lanes(1)
    part = lane % 4
    own = own_ref[...]
    outer = jnp.where(part < 2, unsent(west_ref), unsent(east_ref))
    from_west = jnp.where(part == 1, pltpu.roll(outer, 1, 1), pltpu.roll(own, 1, 1))
    from_east = jnp.where(part == 1, pltpu.roll(own, B - 1, 1), pltpu.roll(outer, B - 1, 1))
    beyond = from_west + from_east + around_rows(outer) - 4.0 * outer
    outer, beyond = swapped(outer, part), swapped(beyond, part)
    ring = lax.broadcasted_iota(jnp.int32, (ROWS, B), 0)
    keep = jnp.where(
        ring == ROWS - 1, ends_ref[0].astype(F32), jnp.where(ring == OY, ends_ref[1].astype(F32), 1.0)
    )
    wide = lanes(ROWS)

    def laplace(v, cols, f):
        edge = pltpu.roll(cols, B - 2 - 4 * f, 1)
        side = jnp.where(wide == 0, edge, pltpu.roll(v, 1, 1)) + jnp.where(
            wide == B - 1, edge, pltpu.roll(v, B - 1, 1)
        )
        return side + around_rows(v) - 4.0 * v

    for f in range(FLD):
        v = circular(flux_ref, north_ref, south_ref, f)
        once = keep * laplace(v, outer, f)
        twice = laplace(once, beyond, f)
        terms[f] = v[0:OY]
        terms[FLD + f] = once[0:OY]
        terms[2 * FLD + f] = twice[0:OY]

    tall = 32
    copies = []
    for i in range(OY // tall):
        rows = pl.ds(i * tall, tall)
        sea = mask_ref[rows, :].astype(F32)
        held = [terms[j, rows, :] for j in range(3 * FLD)]

        def one(level, carry):
            v = x_ref[level, rows, :]
            for j in range(3 * FLD):
                v = v + coef_ref[j, level] * held[j]
            out_ref[level, rows, :] = v * sea
            return carry

        lax.fori_loop(0, LO, one, 0, unroll=5)
        copies.append(pltpu.make_async_copy(out_ref.at[:, rows], out_hbm.at[:, rows], sems.at[i]))
        copies[-1].start()
    for c in copies:
        c.wait()


def apply_flux(coefs, ends, x, mask, flux, north, south, own, west, east):
    return pl.pallas_call(
        apply_flux_kernel,
        in_specs=[SMEM, SMEM] + [VMEM] * 8,
        out_specs=ANY,
        out_shape=f32(LO, OY, B),
        scratch_shapes=[
            pltpu.VMEM((3 * FLD, OY, B), F32),
            pltpu.VMEM((LO, OY, B), F32),
            pltpu.SemaphoreType.DMA((2,)),
        ],
        compiler_params=params(16),
        name="apply_flux",
    )(coefs, ends, x, mask, flux, north, south, own, west, east)


def swap_rows(low_rows, high_rows):
    count = lax.axis_size("face")
    south_going = [(i, i + 1) for i in range(count - 1)]
    north_going = [(i + 1, i) for i in range(count - 1)]
    north = lax.ppermute(high_rows, "face", south_going)
    south = lax.ppermute(low_rows, "face", north_going)
    return north, south


def swap_columns(for_east, for_west):
    count = lax.axis_size("tile")
    east_going = [(i, (i + 1) % count) for i in range(count)]
    west_going = [((i + 1) % count, i) for i in range(count)]
    west = lax.ppermute(for_east, "tile", east_going)
    east = lax.ppermute(for_west, "tile", west_going)
    return west, east


def exchange(rows):
    return lax.all_to_all(rows, ("face", "tile"), split_axis=0, concat_axis=0, tiled=True)


def mix_levels(v, k):
    flow = k[None, :] * (v[:, 1:] - v[:, :-1])
    return v + jnp.pad(flow, ((0, 0), (0, 1))) - jnp.pad(flow, ((0, 0), (1, 0)))


def local(
    atm_tangent,
    atm_mixing,
    flux_coef,
    remap_weight,
    target_device,
    target_row,
    ocean_tangent,
    ocean_mixing,
    penetration,
    sea_mask,
    ocean_adjoint,
):
    face = lax.axis_index("face")
    ends = jnp.stack([face > 0, face < lax.axis_size("face") - 1]).astype(jnp.int32)
    pen = penetration.T
    north, south = swap_rows(*edge_rows(ocean_adjoint, ocean_tangent, sea_mask))
    pair = surface_flux(flux_coef, atm_tangent, atm_mixing)
    pair, north, south = lax.optimization_barrier((pair, north, south))
    own, for_east, for_west = pack_columns(ocean_adjoint, ocean_tangent, sea_mask, north, south)
    pair, for_east, for_west = lax.optimization_barrier((pair, for_east, for_west))
    west, east = swap_columns(for_east, for_west)
    sent, slots = remap(target_device.T, target_row.T, pair, remap_weight)
    sent, west, east = lax.optimization_barrier((sent, west, east))
    arrived = exchange(sent.reshape(DEV, 1, MSG * B)).reshape(DEV * MSG, B)
    ocean_backward, flux_adjoint = ocean_steps(
        True, ocean_mixing, ends, pen, ocean_adjoint, sea_mask, north, south, own, west, east
    )
    (stepped,) = ocean_steps(
        False, ocean_mixing, ends, pen, ocean_tangent, sea_mask, north, south, own, west, east
    )
    flux_adjoint, stepped = lax.optimization_barrier((flux_adjoint, stepped))
    returned = exchange(answer(arrived, flux_adjoint).reshape(DEV, CAP, FLD, B))
    pen_1 = mix_levels(pen, ocean_mixing)
    pen_2 = mix_levels(pen_1, ocean_mixing)
    coefs = jnp.concatenate([pen_2, (2.0 * HRATE) * pen_1, (HRATE * HRATE) * pen], axis=0)
    flux, low, high = collect(arrived)
    f_north, f_south = swap_rows(low, high)
    f_own, f_sent = flux_columns(flux, f_north, f_south)
    f_west, f_east = swap_columns(f_sent, f_sent)
    ocean_forward = apply_flux(
        coefs, ends, stepped, sea_mask, flux, f_north, f_south, f_own, f_west, f_east
    )
    atm = atm_adjoint(
        slots, flux_coef, returned.reshape(DEV * CAP, FLD, B), atm_mixing, remap_weight
    )
    return ocean_forward, ocean_backward, atm


def solution(mesh):
    placed = (
        P(None, ("face", "tile")),
        P(None, ("face", "tile")),
        P(),
        P(("face", "tile"), None, None),
        P(("face", "tile"), None),
        P(("face", "tile"), None),
        P(None, "face", "tile"),
        P(),
        P(),
        P("face", "tile"),
        P(None, "face", "tile"),
    )
    return jax.shard_map(
        local,
        mesh=mesh,
        in_specs=placed,
        out_specs=(P(None, "face", "tile"), P(None, "face", "tile"), P(None, ("face", "tile"))),
        check_vma=False,
    )
```

```python
import functools

import jax
import jax.numpy as jnp
from jax import lax
from jax.experimental import pallas as pl
from jax.experimental.pallas import tpu as pltpu
from jax.sharding import PartitionSpec as P

ATM_SWEEPS = 4
HRATE = 0.1
LA = 64
LO = 75
FLD = 4
B = 128
NBA = 64
KO = 4
OY = 64
CAP = 4
DEV = 128
MSG = CAP * FLD + 1
PIECES = 64
LOT = KO * FLD + 1
GRP = 8
STEPS = NBA // GRP
PLANES = 3
ROWS = 72
TOP = 16
TALL = 96
LEVELS = 25
F32 = jnp.float32
BF16 = jnp.bfloat16
MIB = 1024 * 1024
SMEM = pl.BlockSpec(memory_space=pltpu.SMEM)
VMEM = pl.BlockSpec(memory_space=pltpu.VMEM)
ANY = pl.BlockSpec(memory_space=pl.ANY)
PITCH = LA + 1


def params(mib):
    return pltpu.CompilerParams(vmem_limit_bytes=mib * MIB)


def in_hbm(v):
    return pltpu.with_memory_space_constraint(v, pltpu.HBM)


def f32(*shape):
    return jax.ShapeDtypeStruct(shape, F32)


def split2(v):
    hi = v.astype(BF16)
    return hi, (v - hi.astype(F32)).astype(BF16)


def dot(a, b, dims=((1,), (0,))):
    return lax.dot_general(a, b, (dims, ((), ())), preferred_element_type=F32)


def lanes(rows):
    return lax.broadcasted_iota(jnp.int32, (rows, B), 1)


def sweep_levels(load, mixing, emit):
    values = [{} for _ in range(ATM_SWEEPS + 1)]
    flows = [{} for _ in range(ATM_SWEEPS)]
    mix = {}
    for t in range(LA + ATM_SWEEPS):
        if t < LA:
            values[0][t] = load(t)
            if t < LA - 1:
                mix[t] = mixing(t)
        for s in range(ATM_SWEEPS):
            l = t - 1 - s
            if not 0 <= l < LA:
                continue
            v = values[s][l]
            done = v
            if l < LA - 1:
                flows[s][l] = mix[l] * (values[s][l + 1] - v)
                done = done + flows[s][l]
            if l > 0:
                done = done - flows[s][l - 1]
            values[s + 1][l] = done
            if s == ATM_SWEEPS - 1:
                emit(l, done)


def level_rows(ref, level):
    return ref[pl.ds(level, GRP, stride=PITCH), :]


def block_lanes(block):
    return pl.ds(pl.multiple_of(block * B, B), B)


def square(w_ref, block, k):
    at = block * KO + k
    return jnp.concatenate(
        [
            jnp.concatenate([w_ref[at], w_ref[at + 1]], axis=1),
            jnp.concatenate([w_ref[at + KO], w_ref[at + KO + 1]], axis=1),
        ],
        axis=0,
    )


def surface_flux_kernel(coef_ref, x_ref, mix_ref, out_ref, xs, ms):
    def work(step, carry):
        for b in range(GRP):
            at = block_lanes(step * GRP + b)
            xs[step % 2, pl.ds(b * PITCH, LA), :] = x_ref[:, at]
            ms[step % 2, pl.ds(b * PITCH, LA - 1), :] = mix_ref[:, at].astype(F32)
        sums = [None] * FLD

        def emit(level, v):
            for f in range(FLD):
                term = coef_ref[f, level] * v
                sums[f] = term if sums[f] is None else sums[f] + term

        sweep_levels(
            lambda l: level_rows(xs.at[step % 2], l), lambda l: level_rows(ms.at[step % 2], l), emit
        )
        for f in range(FLD):
            high = sums[f].astype(BF16).astype(F32)
            at = step * GRP * 2 * FLD + f
            out_ref[pl.ds(at, GRP, stride=2 * FLD), :] = high
            out_ref[pl.ds(at + FLD, GRP, stride=2 * FLD), :] = sums[f] - high
        return carry

    lax.fori_loop(0, STEPS, work, 0, unroll=2)


def surface_flux(coef, x, mix):
    return pl.pallas_call(
        surface_flux_kernel,
        in_specs=[SMEM, VMEM, VMEM],
        out_specs=VMEM,
        out_shape=f32(NBA * 2 * FLD, B),
        scratch_shapes=[pltpu.VMEM((2, GRP * PITCH, B), F32), pltpu.VMEM((2, GRP * PITCH, B), F32)],
        compiler_params=params(12),
        name="surface_flux",
    )(coef, x, mix)


def columns_of(rows):
    count, length = rows.shape
    wide = jnp.concatenate([rows, jnp.zeros((count, B - length), F32)], axis=1)
    return jnp.concatenate([wide, jnp.zeros((B - count, B), F32)], axis=0).T[0:length]


def label_rows(td_ref, tr_ref, parts, tiles):
    dev = td_ref[...]
    dev_cols = columns_of(dev.astype(F32))
    row_cols = columns_of(tr_ref[...].astype(F32) + 1.0)
    east = dev // tiles * tiles + (dev + 1) % tiles
    west = dev // tiles * tiles + (dev + tiles - 1) % tiles
    lane = lanes(NBA)
    earlier = (
        lax.broadcasted_iota(jnp.int32, (NBA, NBA), 1) < lax.broadcasted_iota(jnp.int32, (NBA, NBA), 0)
    )
    owner = lax.broadcasted_iota(jnp.int32, (DEV, NBA), 0)
    total = jnp.zeros((DEV, B), F32)
    for k in range(KO):
        mine = dev_cols[:, k : k + 1]
        same = jnp.zeros((NBA, NBA), F32)
        for other in range(KO):
            same = same + (mine == dev[other : other + 1].astype(F32)).astype(F32)
        place = jnp.sum(jnp.where(earlier, same, 0.0), axis=1, keepdims=True).astype(jnp.int32)
        label = row_cols[:, k : k + 1]
        piece = jnp.zeros((NBA, B), F32)
        for f in range(FLD):
            v = parts[pl.ds(k * FLD + f, NBA, stride=LOT), :]
            piece = jnp.where(lane // 4 == f, pltpu.roll(v, 4 * f + 2, 1), piece)
        piece = piece + pltpu.roll(piece, 16, 1)
        piece = pltpu.roll(piece + pltpu.roll(piece, 32, 1), PIECES, 1)
        piece = jnp.where(lane // 16 == PIECES // 16 + place, piece, 0.0)
        own = jnp.where(lane == place, label, 0.0)
        to_east = jnp.where(lane == 4 + place, label, jnp.where(lane % 4 < 2, piece, 0.0))
        to_west = jnp.where(lane == 8 + place, label, jnp.where(lane % 4 < 2, 0.0, piece))
        picks = [
            (owner == d[k : k + 1]).astype(F32).astype(BF16) for d in (dev, east, west)
        ]
        hi, lo = split2(jnp.concatenate([own, to_east, to_west], axis=0))
        pick = jnp.concatenate(picks, axis=1)
        total = total + dot(pick, hi) + dot(pick, lo)
    return total


def remap_kernel(tiles, td_ref, td_rows, tr_rows, pair_ref, w_ref, out_ref, slot_ref, count, parts):
    out_ref[...] = jnp.zeros_like(out_ref)

    def clear(d, c):
        count[d] = 0
        return c

    lax.fori_loop(0, DEV, clear, 0, unroll=8)
    upper = lax.broadcasted_iota(jnp.int32, (4 * FLD, B), 0) < 2 * FLD

    def work(step, carry):
        for i in range(0, GRP, 2):
            row = step * GRP + i
            both = pair_ref[pl.ds(pl.multiple_of(row * 2 * FLD, 4 * FLD), 4 * FLD), :]
            lhs = jnp.concatenate(
                [jnp.where(upper, both, 0.0), jnp.where(upper, 0.0, both)], axis=1
            ).astype(BF16)
            ats = {}
            for a in range(2):
                for k in range(KO):
                    dev = td_ref[k, row + a]
                    place = count[dev]
                    count[dev] = place + 1
                    slot_ref[(row + a) * KO + k] = dev * CAP + place
                    ats[a, k] = dev * MSG + place * FLD
            for k in range(0, KO, 2):
                moved = dot(lhs, square(w_ref, row, k))
                for a in range(2):
                    total = moved[8 * a : 8 * a + 4] + moved[8 * a + 4 : 8 * a + 8]
                    for b in range(2):
                        half = total[:, b * B : (b + 1) * B]
                        out_ref[pl.ds(ats[a, k + b], FLD), :] = half
                        parts[pl.ds((row + a) * LOT + (k + b) * FLD, FLD), :] = half
        return carry

    lax.fori_loop(0, STEPS, work, 0, unroll=STEPS)
    out_ref[pl.ds(MSG - 1, DEV, stride=MSG), :] = label_rows(td_rows, tr_rows, parts, tiles)


def remap(tiles, td, tr, pair, w):
    return pl.pallas_call(
        functools.partial(remap_kernel, tiles),
        in_specs=[SMEM] + [VMEM] * 4,
        out_specs=[VMEM, SMEM],
        out_shape=[pltpu.HBM((DEV * MSG, B), F32), jax.ShapeDtypeStruct((NBA * KO,), jnp.int32)],
        scratch_shapes=[pltpu.SMEM((DEV,), jnp.int32), pltpu.VMEM((NBA * LOT, B), F32)],
        compiler_params=params(16),
        name="remap",
    )(td, td, tr, pair, w)


def atm_adjoint_kernel(
    slot_ref, coef_ref, back_ref, mix_ref, w_hbm, out_hbm, w_ref, ms, total_ref, steps_ref, out_ref, sems
):
    cols = GRP * B

    def w_copy(s):
        part = pl.ds(s * GRP * KO, GRP * KO)
        return pltpu.make_async_copy(w_hbm.at[part], w_ref.at[part], sems.at[0, s])

    def out_copy(s):
        part = pl.ds(pl.multiple_of(s * cols, cols), cols)
        return pltpu.make_async_copy(out_ref.at[:, part], out_hbm.at[:, part], sems.at[1, s])

    for s in range(STEPS):
        w_copy(s).start()

    def work(step, carry):
        w_copy(step).wait()
        for i in range(0, GRP, 2):
            row = step * GRP + i
            total = None
            for k in range(0, KO, 2):
                blocks = []
                for a in range(2):
                    pieces = []
                    for b in range(2):
                        v = back_ref[slot_ref[(row + a) * KO + k + b]]
                        high = v.astype(BF16).astype(F32)
                        pieces.append(jnp.concatenate([high, v - high], axis=0))
                    blocks.append(jnp.concatenate(pieces, axis=1))
                lhs = jnp.concatenate(blocks, axis=0).astype(BF16)
                part = dot(lhs, square(w_ref, row, k), ((1,), (1,)))
                total = part if total is None else total + part
            total_ref[pl.ds(i * FLD, FLD), :] = total[0:4, 0:B] + total[4:8, 0:B]
            total_ref[pl.ds((i + 1) * FLD, FLD), :] = total[8:12, B:] + total[12:16, B:]
        for b in range(GRP):
            ms[pl.ds(b * PITCH, LA - 1), :] = mix_ref[:, block_lanes(step * GRP + b)].astype(F32)
        fields = [total_ref[pl.ds(f, GRP, stride=FLD), :] for f in range(FLD)]

        def load(level):
            v = coef_ref[0, level] * fields[0]
            for f in range(1, FLD):
                v = v + coef_ref[f, level] * fields[f]
            return v

        def emit(level, v):
            steps_ref[pl.ds(level, GRP, stride=PITCH), :] = v

        sweep_levels(load, lambda l: level_rows(ms, l), emit)
        for b in range(GRP):
            out_ref[:, block_lanes(step * GRP + b)] = steps_ref[pl.ds(b * PITCH, LA), :]
        out_copy(step).start()
        return carry

    lax.fori_loop(0, STEPS, work, 0, unroll=2)
    for s in range(STEPS):
        out_copy(s).wait()


def atm_adjoint(slots, coef, back, mix, w):
    return pl.pallas_call(
        atm_adjoint_kernel,
        in_specs=[SMEM, SMEM, VMEM, VMEM, ANY],
        out_specs=ANY,
        out_shape=f32(LA, NBA * B),
        scratch_shapes=[
            pltpu.VMEM((NBA * KO, B, B), BF16),
            pltpu.VMEM((GRP * PITCH, B), F32),
            pltpu.VMEM((GRP * FLD, B), F32),
            pltpu.VMEM((GRP * PITCH, B), F32),
            pltpu.VMEM((LA, NBA * B), F32),
            pltpu.SemaphoreType.DMA((2, STEPS)),
        ],
        compiler_params=params(24),
        name="atm_adjoint",
    )(slots, coef, back, mix, in_hbm(w))


def rows_kernel(a_hbm, t_hbm, m_hbm, low_ref, high_ref, a_ref, t_ref, m_ref, sems):
    copies = []
    for i, r in enumerate((0, OY - 8)):
        rows = pl.ds(r, 8)
        copies += [
            pltpu.make_async_copy(a_hbm.at[:, rows], a_ref.at[i], sems.at[0, i]),
            pltpu.make_async_copy(t_hbm.at[:, rows], t_ref.at[i], sems.at[1, i]),
            pltpu.make_async_copy(m_hbm.at[rows], m_ref.at[i], sems.at[2, i]),
        ]
    for c in copies:
        c.start()
    for c in copies:
        c.wait()
    low_ref[0:LO] = a_ref[0, :, 0:2, :] * m_ref[0, 0:2].astype(F32)
    low_ref[LO:] = t_ref[0, :, 0:2, :]
    high_ref[0:LO] = a_ref[1, :, 6:8, :] * m_ref[1, 6:8].astype(F32)
    high_ref[LO:] = t_ref[1, :, 6:8, :]


def edge_rows(adjoint, tangent, mask):
    return pl.pallas_call(
        rows_kernel,
        in_specs=[ANY] * 3,
        out_specs=[VMEM, VMEM],
        out_shape=[f32(2 * LO, 2, B), f32(2 * LO, 2, B)],
        scratch_shapes=[
            pltpu.VMEM((2, LO, 8, B), F32),
            pltpu.VMEM((2, LO, 8, B), F32),
            pltpu.VMEM((2, 8, B), jnp.int32),
            pltpu.SemaphoreType.DMA((3, 2)),
        ],
        compiler_params=params(8),
        name="edge_rows",
    )(in_hbm(adjoint), in_hbm(tangent), in_hbm(mask))


def level_lanes(plane):
    return range(min(32, LO - 32 * plane))


def pack_kernel(a_ref, t_ref, mask_ref, north_ref, south_ref, own_ref, east_ref, west_ref):
    sea = mask_ref[...].astype(F32)
    lane = lanes(1)
    part = lane % 4
    for plane in range(PLANES):
        held = []
        for at, x_ref in ((0, a_ref), (LO, t_ref)):
            body = jnp.zeros((OY, B), F32)
            rim = jnp.zeros((2, B), F32)
            for m in level_lanes(plane):
                level = 32 * plane + m
                mine = lane // 4 == m
                body = jnp.where(mine, pltpu.roll(x_ref[level], (4 * m + 2) % B, 1), body)
                edge = jnp.concatenate(
                    [south_ref[at + level, 0:1], north_ref[at + level, 1:2]], axis=0
                )
                rim = jnp.where(mine, pltpu.roll(edge, (4 * m + 2) % B, 1), rim)
            if at == 0:
                body = body * jnp.where(part < 2, edge_mask(sea, part, True), edge_mask(sea, part, False))
            held.append(
                jnp.concatenate([body, rim[0:1], jnp.zeros((6, B), F32), rim[1:2]], axis=0)
            )
        adj, tan = held
        own_ref[0, plane] = adj
        own_ref[1, plane] = tan
        east_ref[plane] = jnp.where(part < 2, adj, pltpu.roll(tan, 2, 1))
        west_ref[plane] = jnp.where(part < 2, pltpu.roll(adj, B - 2, 1), tan)


def edge_mask(sea, part, high):
    first = B - 2 if high else 0
    return jnp.where(part % 2 == 0, sea[:, first : first + 1], sea[:, first + 1 : first + 2])


def pack_columns(adjoint, tangent, mask, north, south):
    return pl.pallas_call(
        pack_kernel,
        out_shape=[f32(2, PLANES, ROWS, B), f32(PLANES, ROWS, B), f32(PLANES, ROWS, B)],
        compiler_params=params(12),
        name="pack_columns",
    )(adjoint, tangent, mask, north, south)


def lateral_table():
    r = lax.broadcasted_iota(jnp.int32, (B, B), 0)
    c = lax.broadcasted_iota(jnp.int32, (B, B), 1)
    near = ((r - c == 1) | (c - r == 1)).astype(F32).astype(BF16)
    return jnp.concatenate([near, near], axis=0)


def swapped(v, part):
    return jnp.where(part == 2, pltpu.roll(v, 1, 1), pltpu.roll(v, B - 1, 1))


def around_rows(v):
    return pltpu.roll(v, 1, 0) + pltpu.roll(v, ROWS - 1, 0)


def ocean_kernel(adjoint, k_ref, ends_ref, pen_ref, x_ref, mask_ref, north_ref, south_ref,
                 own_ref, west_ref, east_ref, *rest):
    if adjoint:
        out_hbm, flux_ref, state, first, fix, out_ref, sem = rest
    else:
        out_hbm, state, first, fix, out_ref, sem = rest
    sea = mask_ref[...].astype(F32)

    state[:, 8:TOP, :] = jnp.zeros((LO + 1, 8, B), F32)
    state[:, TOP + OY : TOP + OY + 8, :] = jnp.zeros((LO + 1, 8, B), F32)
    state[0:LO, TOP - 2 : TOP, :] = north_ref[...]
    state[0:LO, TOP + OY : TOP + OY + 2, :] = south_ref[...]
    state[LO, TOP : TOP + OY] = jnp.zeros((OY, B), F32)

    def fill(level, carry):
        v = x_ref[level]
        state[level, TOP : TOP + OY] = v * sea if adjoint else v
        return carry

    lax.fori_loop(0, LO, fill, 0, unroll=5)

    lane = lanes(1)
    part = lane % 4
    ups, downs = [], []
    for plane in range(PLANES):
        up = jnp.zeros((1, B), F32)
        down = jnp.zeros((1, B), F32)
        for m in level_lanes(plane):
            level = 32 * plane + m
            mine = lane // 4 == m
            if level < LO - 1:
                up = jnp.where(mine, k_ref[level], up)
            if level > 0:
                down = jnp.where(mine, k_ref[level - 1], down)
        ups.append(up)
        downs.append(down)
    own = [own_ref[0, p] for p in range(PLANES)]
    if adjoint:
        outer = [
            jnp.where(part < 2, west_ref[p], pltpu.roll(east_ref[p], 2, 1)) for p in range(PLANES)
        ]
    else:
        outer = [
            jnp.where(part < 2, pltpu.roll(west_ref[p], B - 2, 1), east_ref[p])
            for p in range(PLANES)
        ]

    def vertical(vs, p):
        c = vs[p]
        higher = pltpu.roll(c, B - 4, 1)
        if p + 1 < PLANES:
            higher = jnp.where(lane < B - 4, higher, pltpu.roll(vs[p + 1], B - 4, 1))
        lower = pltpu.roll(c, 4, 1)
        if p > 0:
            lower = jnp.where(lane >= 4, lower, pltpu.roll(vs[p - 1], 4, 1))
        return c + ups[p] * (higher - c) - downs[p] * (c - lower)

    inner = (part == 1) | (part == 2)
    added = [jnp.where(inner, HRATE * swapped(c, part), 0.0) for c in outer]
    for p in range(PLANES):
        c = outer[p]
        from_west = jnp.where(part == 1, pltpu.roll(c, 1, 1), pltpu.roll(own[p], 1, 1))
        from_east = jnp.where(part == 1, pltpu.roll(own[p], B - 1, 1), pltpu.roll(c, B - 1, 1))
        beyond = vertical(outer, p) + HRATE * (from_west + from_east + around_rows(c) - 4.0 * c)
        e = added[p]
        side = HRATE * (pltpu.roll(e, B - 1, 1) + pltpu.roll(e, 1, 1))
        here = vertical(added, p) + HRATE * (around_rows(e) - 4.0 * e + swapped(beyond, part))
        fix[p] = jnp.where(inner, here, side)[0:OY]

    table = lateral_table()
    first[LO] = jnp.zeros((TALL, B), F32)
    row = lax.broadcasted_iota(jnp.int32, (OY + 16, B), 0) + 8
    keep = jnp.where(
        row == TOP - 1, ends_ref[0].astype(F32), jnp.where(row == TOP + OY, ends_ref[1].astype(F32), 1.0)
    )
    wide = lanes(OY)
    edge_lane = (wide < 2) | (wide >= B - 2)

    def step(src, start, count, second):
        rows = pl.ds(start, count)

        def body(group, below):
            base = group * LEVELS
            vs = [src[base + j, rows, :] for j in range(LEVELS + 1)]
            hi, lo = split2(jnp.concatenate(vs[:LEVELS], axis=0))
            side = dot(jnp.concatenate([hi, lo], axis=1), table)
            for j in range(LEVELS):
                level = base + j
                v = vs[j]
                k = jnp.where(level < LO - 1, k_ref[jnp.minimum(level, LO - 2)], 0.0)
                flow = k * (vs[j + 1] - v)
                near = (
                    src[level, pl.ds(start - 1, count), :]
                    + src[level, pl.ds(start + 1, count), :]
                    + side[j * count : (j + 1) * count]
                )
                done = v * (1.0 - 4.0 * HRATE) + (flow - below) + HRATE * near
                if second:
                    shift = (2 * B - 2 - 4 * (level % 32)) % B
                    extra = pltpu.roll(fix[level // 32], shift, 1)
                    done = done + jnp.where(edge_lane, extra, 0.0)
                    out_ref[level] = done
                else:
                    first[level, rows, :] = done * keep
                below = flow
            return below

        lax.fori_loop(0, LO // LEVELS, body, jnp.zeros((count, B), F32))

    step(state, 8, OY + 16, False)
    step(first, TOP, OY, True)
    out_copy = pltpu.make_async_copy(out_ref, out_hbm, sem.at[0])
    out_copy.start()

    if adjoint:
        tall = 32
        for r in range(0, OY, tall):
            rows = pl.ds(r, tall)

            def project(level, sums):
                v = out_ref[level, rows, :]
                return tuple(s + pen_ref[f, level] * v for f, s in enumerate(sums))

            sums = lax.fori_loop(
                0, LO, project, tuple(jnp.zeros((tall, B), F32) for _ in range(FLD)), unroll=5
            )
            for f in range(FLD):
                flux_ref[rows, f * B : (f + 1) * B] = sums[f]
    out_copy.wait()


def ocean_steps(adjoint, k, ends, pen, x, mask, north, south, own, west, east):
    at = 0 if adjoint else 1
    rim = pl.BlockSpec((LO, 2, B), lambda i: (at, 0, 0))
    full = lambda *shape: pl.BlockSpec(shape, lambda i: (0,) * len(shape))
    shapes = [f32(LO, OY, B)]
    outs = [ANY]
    if adjoint:
        shapes.append(f32(OY, FLD * B))
        outs.append(full(OY, FLD * B))
    return pl.pallas_call(
        functools.partial(ocean_kernel, adjoint),
        grid=(1,),
        in_specs=[
            SMEM,
            SMEM,
            SMEM,
            full(LO, OY, B),
            full(OY, B),
            rim,
            rim,
            pl.BlockSpec((1, PLANES, ROWS, B), lambda i: (at, 0, 0, 0)),
            full(PLANES, ROWS, B),
            full(PLANES, ROWS, B),
        ],
        out_specs=outs,
        out_shape=shapes,
        scratch_shapes=[
            pltpu.VMEM((LO + 1, TALL, B), F32),
            pltpu.VMEM((LO + 1, TALL, B), F32),
            pltpu.VMEM((PLANES, OY, B), F32),
            pltpu.VMEM((LO, OY, B), F32),
            pltpu.SemaphoreType.DMA((1,)),
        ],
        compiler_params=params(24),
        name="ocean_adjoint" if adjoint else "ocean_tangent",
    )(k, ends, pen, x, mask, north, south, own, west, east)


def answer_kernel(msg_ref, flux_ref, out_ref):
    labels = msg_ref[pl.ds(MSG - 1, DEV, stride=MSG), :]
    gh, gl = split2(flux_ref[...])
    table = jnp.concatenate([gh, gl], axis=0)
    want = lax.broadcasted_iota(jnp.int32, (DEV, B), 1) % OY + 1
    for c in range(CAP):
        pick = (labels[:, c : c + 1].astype(jnp.int32) == want).astype(F32).astype(BF16)
        rows = dot(pick, table)
        for f in range(FLD):
            out_ref[pl.ds(c * FLD + f, DEV, stride=CAP * FLD), :] = rows[:, f * B : (f + 1) * B]


def answer(msg, flux):
    return pl.pallas_call(
        answer_kernel,
        out_shape=f32(DEV * CAP * FLD, B),
        compiler_params=params(12),
        name="answer",
    )(msg, flux)


def collect_kernel(msg_ref, flux_ref, outer_ref, low_ref, high_ref):
    last = msg_ref[pl.ds(MSG - 1, DEV, stride=MSG), :]
    labels = last.T.astype(jnp.int32)
    rows = lax.broadcasted_iota(jnp.int32, (OY, DEV), 0) + 1

    def picked(at):
        return (labels[at : at + 1, :] == rows).astype(F32).astype(BF16)

    lane = lanes(DEV)
    first_lot = lane < 4 * FLD
    total = jnp.zeros((OY, FLD * B), F32)
    outer = jnp.zeros((OY, B), F32)
    for c in range(CAP):
        pick = picked(c)
        data = jnp.concatenate(
            [msg_ref[pl.ds(c * FLD + f, DEV, stride=MSG), :] for f in range(FLD)], axis=1
        )
        dh, dl = split2(data)
        total = total + dot(jnp.concatenate([pick, pick], axis=1), jnp.concatenate([dh, dl], axis=0))
        piece = jnp.where(first_lot, pltpu.roll(last, (2 * B - PIECES - 16 * c) % B, 1), 0.0)
        west = jnp.where(lane % 4 < 2, piece, 0.0)
        wh, wl = split2(west)
        eh, el = split2(piece - west)
        west_pick, east_pick = picked(4 + c), picked(8 + c)
        outer = outer + dot(
            jnp.concatenate([west_pick, west_pick, east_pick, east_pick], axis=1),
            jnp.concatenate([wh, wl, eh, el], axis=0),
        )
    outer_ref[...] = outer
    for f in range(FLD):
        v = total[:, f * B : (f + 1) * B]
        flux_ref[f] = v
        low_ref[f] = v[0:2]
        high_ref[f] = v[OY - 2 : OY]
    low_ref[FLD] = outer[0:2]
    high_ref[FLD] = outer[OY - 2 : OY]


def collect(msg):
    return pl.pallas_call(
        collect_kernel,
        out_shape=[f32(FLD, OY, B), f32(OY, B), f32(FLD + 1, 2, B), f32(FLD + 1, 2, B)],
        compiler_params=params(12),
        name="collect",
    )(msg)


def circular(own, north, south):
    return jnp.concatenate([own, south, jnp.zeros((ROWS - OY - 4, B), F32), north], axis=0)


def apply_flux_kernel(
    coef_ref, ends_ref, x_ref, mask_ref, flux_ref, outer_ref, north_ref, south_ref,
    out_hbm, terms, out_ref, sems
):
    lane = lanes(1)
    part = lane % 4
    planes = [circular(flux_ref[f], north_ref[f], south_ref[f]) for f in range(FLD)]
    own = jnp.zeros((ROWS, B), F32)
    for f in range(FLD):
        own = jnp.where(lane // 4 == f, pltpu.roll(planes[f], 4 * f + 2, 1), own)
    outer = circular(outer_ref[...], north_ref[FLD], south_ref[FLD])
    from_west = jnp.where(part == 1, pltpu.roll(outer, 1, 1), pltpu.roll(own, 1, 1))
    from_east = jnp.where(part == 1, pltpu.roll(own, B - 1, 1), pltpu.roll(outer, B - 1, 1))
    beyond = from_west + from_east + around_rows(outer) - 4.0 * outer
    outer, beyond = swapped(outer, part), swapped(beyond, part)
    ring = lax.broadcasted_iota(jnp.int32, (ROWS, B), 0)
    keep = jnp.where(
        ring == ROWS - 1, ends_ref[0].astype(F32), jnp.where(ring == OY, ends_ref[1].astype(F32), 1.0)
    )
    wide = lanes(ROWS)

    def laplace(v, cols, f):
        edge = pltpu.roll(cols, B - 2 - 4 * f, 1)
        side = jnp.where(wide == 0, edge, pltpu.roll(v, 1, 1)) + jnp.where(
            wide == B - 1, edge, pltpu.roll(v, B - 1, 1)
        )
        return side + around_rows(v) - 4.0 * v

    for f in range(FLD):
        v = planes[f]
        once = keep * laplace(v, outer, f)
        twice = laplace(once, beyond, f)
        terms[f] = v[0:OY]
        terms[FLD + f] = once[0:OY]
        terms[2 * FLD + f] = twice[0:OY]

    tall = 32
    copies = []
    for i in range(OY // tall):
        rows = pl.ds(i * tall, tall)
        sea = mask_ref[rows, :].astype(F32)
        held = [terms[j, rows, :] for j in range(3 * FLD)]

        def one(level, carry):
            v = x_ref[level, rows, :]
            for j in range(3 * FLD):
                v = v + coef_ref[j, level] * held[j]
            out_ref[level, rows, :] = v * sea
            return carry

        lax.fori_loop(0, LO, one, 0, unroll=5)
        copies.append(pltpu.make_async_copy(out_ref.at[:, rows], out_hbm.at[:, rows], sems.at[i]))
        copies[-1].start()
    for c in copies:
        c.wait()


def apply_flux(coefs, ends, x, mask, flux, outer, north, south):
    return pl.pallas_call(
        apply_flux_kernel,
        in_specs=[SMEM, SMEM] + [VMEM] * 6,
        out_specs=ANY,
        out_shape=f32(LO, OY, B),
        scratch_shapes=[
            pltpu.VMEM((3 * FLD, OY, B), F32),
            pltpu.VMEM((LO, OY, B), F32),
            pltpu.SemaphoreType.DMA((2,)),
        ],
        compiler_params=params(16),
        name="apply_flux",
    )(coefs, ends, x, mask, flux, outer, north, south)


def swap_rows(low_rows, high_rows):
    count = lax.axis_size("face")
    south_going = [(i, i + 1) for i in range(count - 1)]
    north_going = [(i + 1, i) for i in range(count - 1)]
    north = lax.ppermute(high_rows, "face", south_going)
    south = lax.ppermute(low_rows, "face", north_going)
    return north, south


def swap_columns(for_east, for_west):
    count = lax.axis_size("tile")
    east_going = [(i, (i + 1) % count) for i in range(count)]
    west_going = [((i + 1) % count, i) for i in range(count)]
    west = lax.ppermute(for_east, "tile", east_going)
    east = lax.ppermute(for_west, "tile", west_going)
    return west, east


def exchange(rows):
    return lax.all_to_all(rows, ("face", "tile"), split_axis=0, concat_axis=0, tiled=True)


def mix_levels(v, k):
    flow = k[None, :] * (v[:, 1:] - v[:, :-1])
    return v + jnp.pad(flow, ((0, 0), (0, 1))) - jnp.pad(flow, ((0, 0), (1, 0)))


def local(
    atm_tangent,
    atm_mixing,
    flux_coef,
    remap_weight,
    target_device,
    target_row,
    ocean_tangent,
    ocean_mixing,
    penetration,
    sea_mask,
    ocean_adjoint,
):
    face = lax.axis_index("face")
    ends = jnp.stack([face > 0, face < lax.axis_size("face") - 1]).astype(jnp.int32)
    pen = penetration.T
    north, south = swap_rows(*edge_rows(ocean_adjoint, ocean_tangent, sea_mask))
    pair = surface_flux(flux_coef, atm_tangent, atm_mixing)
    pair, north, south = lax.optimization_barrier((pair, north, south))
    own, for_east, for_west = pack_columns(ocean_adjoint, ocean_tangent, sea_mask, north, south)
    pair, for_east, for_west = lax.optimization_barrier((pair, for_east, for_west))
    west, east = swap_columns(for_east, for_west)
    sent, slots = remap(
        lax.axis_size("tile"), target_device.T, target_row.T, pair, remap_weight
    )
    sent, west, east = lax.optimization_barrier((sent, west, east))
    arrived = exchange(sent.reshape(DEV, 1, MSG * B)).reshape(DEV * MSG, B)
    ocean_backward, flux_adjoint = ocean_steps(
        True, ocean_mixing, ends, pen, ocean_adjoint, sea_mask, north, south, own, west, east
    )
    (stepped,) = ocean_steps(
        False, ocean_mixing, ends, pen, ocean_tangent, sea_mask, north, south, own, west, east
    )
    flux_adjoint, stepped = lax.optimization_barrier((flux_adjoint, stepped))
    returned = exchange(answer(arrived, flux_adjoint).reshape(DEV, CAP, FLD, B))
    pen_1 = mix_levels(pen, ocean_mixing)
    pen_2 = mix_levels(pen_1, ocean_mixing)
    coefs = jnp.concatenate([pen_2, (2.0 * HRATE) * pen_1, (HRATE * HRATE) * pen], axis=0)
    flux, outer, low, high = collect(arrived)
    f_north, f_south = swap_rows(low, high)
    ocean_forward = apply_flux(coefs, ends, stepped, sea_mask, flux, outer, f_north, f_south)
    atm = atm_adjoint(
        slots, flux_coef, returned.reshape(DEV * CAP, FLD, B), atm_mixing, remap_weight
    )
    return ocean_forward, ocean_backward, atm


def solution(mesh):
    placed = (
        P(None, ("face", "tile")),
        P(None, ("face", "tile")),
        P(),
        P(("face", "tile"), None, None),
        P(("face", "tile"), None),
        P(("face", "tile"), None),
        P(None, "face", "tile"),
        P(),
        P(),
        P("face", "tile"),
        P(None, "face", "tile"),
    )
    return jax.shard_map(
        local,
        mesh=mesh,
        in_specs=placed,
        out_specs=(P(None, "face", "tile"), P(None, "face", "tile"), P(None, ("face", "tile"))),
        check_vma=False,
    )
```

```python
import functools

import jax
import jax.numpy as jnp
from jax import lax
from jax.experimental import pallas as pl
from jax.experimental.pallas import tpu as pltpu
from jax.sharding import PartitionSpec as P

ATM_SWEEPS = 4
HRATE = 0.1
LA = 64
LO = 75
FLD = 4
B = 128
NBA = 64
KO = 4
OY = 64
CAP = 4
DEV = 128
MSG = CAP * FLD + 1
PIECES = 64
LOT = KO * FLD + 1
GRP = 8
STEPS = NBA // GRP
PLANES = 3
ROWS = 72
TOP = 16
TALL = 96
LEVELS = 25
F32 = jnp.float32
BF16 = jnp.bfloat16
MIB = 1024 * 1024
SMEM = pl.BlockSpec(memory_space=pltpu.SMEM)
VMEM = pl.BlockSpec(memory_space=pltpu.VMEM)
ANY = pl.BlockSpec(memory_space=pl.ANY)
PITCH = LA + 1


def params(mib):
    return pltpu.CompilerParams(vmem_limit_bytes=mib * MIB)


def cost(us):
    return pl.CostEstimate(
        flops=int(us * 300000000), bytes_accessed=int(us * 900000), transcendentals=0
    )


def in_hbm(v):
    return pltpu.with_memory_space_constraint(v, pltpu.HBM)


def f32(*shape):
    return jax.ShapeDtypeStruct(shape, F32)


def split2(v):
    hi = v.astype(BF16)
    return hi, (v - hi.astype(F32)).astype(BF16)


def dot(a, b, dims=((1,), (0,))):
    return lax.dot_general(a, b, (dims, ((), ())), preferred_element_type=F32)


def lanes(rows):
    return lax.broadcasted_iota(jnp.int32, (rows, B), 1)


def sweep_levels(load, mixing, emit):
    values = [{} for _ in range(ATM_SWEEPS + 1)]
    flows = [{} for _ in range(ATM_SWEEPS)]
    mix = {}
    for t in range(LA + ATM_SWEEPS):
        if t < LA:
            values[0][t] = load(t)
            if t < LA - 1:
                mix[t] = mixing(t)
        for s in range(ATM_SWEEPS):
            l = t - 1 - s
            if not 0 <= l < LA:
                continue
            v = values[s][l]
            done = v
            if l < LA - 1:
                flows[s][l] = mix[l] * (values[s][l + 1] - v)
                done = done + flows[s][l]
            if l > 0:
                done = done - flows[s][l - 1]
            values[s + 1][l] = done
            if s == ATM_SWEEPS - 1:
                emit(l, done)


def level_rows(ref, level):
    return ref[pl.ds(level, GRP, stride=PITCH), :]


def block_lanes(block):
    return pl.ds(pl.multiple_of(block * B, B), B)


def square(w_ref, block, k):
    at = block * KO + k
    return jnp.concatenate(
        [
            jnp.concatenate([w_ref[at], w_ref[at + 1]], axis=1),
            jnp.concatenate([w_ref[at + KO], w_ref[at + KO + 1]], axis=1),
        ],
        axis=0,
    )


def surface_flux_kernel(coef_ref, x_hbm, mix_hbm, out_ref, x_ref, mix_ref, xs, ms, sems):
    cols = GRP * B

    def x_copy(s):
        part = pl.ds(s * cols, cols)
        return pltpu.make_async_copy(x_hbm.at[:, part], x_ref.at[:, part], sems.at[0, s])

    def mix_copy(s):
        part = pl.ds(s * cols, cols)
        return pltpu.make_async_copy(mix_hbm.at[:, part], mix_ref.at[:, part], sems.at[1, s])

    for s in range(STEPS):
        x_copy(s).start()
        mix_copy(s).start()

    def one(step):
        for b in range(GRP):
            at = block_lanes(step * GRP + b)
            xs[step % 2, pl.ds(b * PITCH, LA), :] = x_ref[:, at]
            ms[step % 2, pl.ds(b * PITCH, LA - 1), :] = mix_ref[:, at].astype(F32)
        sums = [None] * FLD

        def emit(level, v):
            for f in range(FLD):
                term = coef_ref[f, level] * v
                sums[f] = term if sums[f] is None else sums[f] + term

        sweep_levels(
            lambda l: level_rows(xs.at[step % 2], l), lambda l: level_rows(ms.at[step % 2], l), emit
        )
        for f in range(FLD):
            high = sums[f].astype(BF16).astype(F32)
            at = step * GRP * 2 * FLD + f
            out_ref[pl.ds(at, GRP, stride=2 * FLD), :] = high
            out_ref[pl.ds(at + FLD, GRP, stride=2 * FLD), :] = sums[f] - high

    def work(pair, carry):
        for half in range(2):
            x_copy(2 * pair + half).wait()
            mix_copy(2 * pair + half).wait()
        for half in range(2):
            one(2 * pair + half)
        return carry

    lax.fori_loop(0, STEPS // 2, work, 0)


def surface_flux(coef, x, mix):
    return pl.pallas_call(
        surface_flux_kernel,
        in_specs=[SMEM, ANY, ANY],
        out_specs=VMEM,
        out_shape=f32(NBA * 2 * FLD, B),
        scratch_shapes=[
            pltpu.VMEM((LA, NBA * B), F32),
            pltpu.VMEM((LA - 1, NBA * B), BF16),
            pltpu.VMEM((2, GRP * PITCH, B), F32),
            pltpu.VMEM((2, GRP * PITCH, B), F32),
            pltpu.SemaphoreType.DMA((2, STEPS)),
        ],
        compiler_params=params(12),
        name="surface_flux",
    )(coef, in_hbm(x), in_hbm(mix))


def columns_of(rows):
    count, length = rows.shape
    wide = jnp.concatenate([rows, jnp.zeros((count, B - length), F32)], axis=1)
    return jnp.concatenate([wide, jnp.zeros((B - count, B), F32)], axis=0).T[0:length]


def label_rows(td_ref, tr_ref, parts, tiles):
    dev = td_ref[...]
    dev_cols = columns_of(dev.astype(F32))
    row_cols = columns_of(tr_ref[...].astype(F32) + 1.0)
    east = dev // tiles * tiles + (dev + 1) % tiles
    west = dev // tiles * tiles + (dev + tiles - 1) % tiles
    lane = lanes(NBA)
    earlier = (
        lax.broadcasted_iota(jnp.int32, (NBA, NBA), 1) < lax.broadcasted_iota(jnp.int32, (NBA, NBA), 0)
    )
    owner = lax.broadcasted_iota(jnp.int32, (DEV, NBA), 0)
    total = jnp.zeros((DEV, B), F32)
    for k in range(KO):
        mine = dev_cols[:, k : k + 1]
        same = jnp.zeros((NBA, NBA), F32)
        for other in range(KO):
            same = same + (mine == dev[other : other + 1].astype(F32)).astype(F32)
        place = jnp.sum(jnp.where(earlier, same, 0.0), axis=1, keepdims=True).astype(jnp.int32)
        label = row_cols[:, k : k + 1]
        piece = jnp.zeros((NBA, B), F32)
        for f in range(FLD):
            v = parts[pl.ds(k * FLD + f, NBA, stride=LOT), :]
            piece = jnp.where(lane // 4 == f, pltpu.roll(v, 4 * f + 2, 1), piece)
        piece = piece + pltpu.roll(piece, 16, 1)
        piece = pltpu.roll(piece + pltpu.roll(piece, 32, 1), PIECES, 1)
        piece = jnp.where(lane // 16 == PIECES // 16 + place, piece, 0.0)
        own = jnp.where(lane == place, label, 0.0)
        to_east = jnp.where(lane == 4 + place, label, jnp.where(lane % 4 < 2, piece, 0.0))
        to_west = jnp.where(lane == 8 + place, label, jnp.where(lane % 4 < 2, 0.0, piece))
        picks = [
            (owner == d[k : k + 1]).astype(F32).astype(BF16) for d in (dev, east, west)
        ]
        hi, lo = split2(jnp.concatenate([own, to_east, to_west], axis=0))
        pick = jnp.concatenate(picks, axis=1)
        total = total + dot(pick, hi) + dot(pick, lo)
    return total


def remap_kernel(tiles, td_ref, td_rows, tr_rows, pair_ref, w_ref, out_ref, slot_ref, count, parts):
    out_ref[...] = jnp.zeros_like(out_ref)

    def clear(d, c):
        count[d] = 0
        return c

    lax.fori_loop(0, DEV, clear, 0, unroll=8)
    upper = lax.broadcasted_iota(jnp.int32, (4 * FLD, B), 0) < 2 * FLD

    def work(step, carry):
        for i in range(0, GRP, 2):
            row = step * GRP + i
            both = pair_ref[pl.ds(pl.multiple_of(row * 2 * FLD, 4 * FLD), 4 * FLD), :]
            lhs = jnp.concatenate(
                [jnp.where(upper, both, 0.0), jnp.where(upper, 0.0, both)], axis=1
            ).astype(BF16)
            ats = {}
            for a in range(2):
                for k in range(KO):
                    dev = td_ref[k, row + a]
                    place = count[dev]
                    count[dev] = place + 1
                    slot_ref[(row + a) * KO + k] = dev * CAP + place
                    ats[a, k] = dev * MSG + place * FLD
            for k in range(0, KO, 2):
                moved = dot(lhs, square(w_ref, row, k))
                for a in range(2):
                    total = moved[8 * a : 8 * a + 4] + moved[8 * a + 4 : 8 * a + 8]
                    for b in range(2):
                        half = total[:, b * B : (b + 1) * B]
                        out_ref[pl.ds(ats[a, k + b], FLD), :] = half
                        parts[pl.ds((row + a) * LOT + (k + b) * FLD, FLD), :] = half
        return carry

    lax.fori_loop(0, STEPS, work, 0, unroll=STEPS)
    out_ref[pl.ds(MSG - 1, DEV, stride=MSG), :] = label_rows(td_rows, tr_rows, parts, tiles)


def remap(tiles, td, tr, pair, w):
    return pl.pallas_call(
        functools.partial(remap_kernel, tiles),
        in_specs=[SMEM] + [VMEM] * 4,
        out_specs=[VMEM, SMEM],
        out_shape=[pltpu.HBM((DEV * MSG, B), F32), jax.ShapeDtypeStruct((NBA * KO,), jnp.int32)],
        scratch_shapes=[pltpu.SMEM((DEV,), jnp.int32), pltpu.VMEM((NBA * LOT, B), F32)],
        compiler_params=params(16),
        name="remap",
    )(td, td, tr, pair, w)


def atm_adjoint_kernel(
    slot_ref, coef_ref, back_ref, mix_ref, w_hbm, out_hbm, w_ref, ms, total_ref, steps_ref, out_ref, sems
):
    cols = GRP * B

    def w_copy(s):
        part = pl.ds(s * GRP * KO, GRP * KO)
        return pltpu.make_async_copy(w_hbm.at[part], w_ref.at[part], sems.at[0, s])

    def out_copy(s):
        part = pl.ds(pl.multiple_of(s * cols, cols), cols)
        return pltpu.make_async_copy(out_ref.at[:, part], out_hbm.at[:, part], sems.at[1, s])

    for s in range(STEPS):
        w_copy(s).start()

    def one(step):
        for i in range(0, GRP, 2):
            row = step * GRP + i
            total = None
            for k in range(0, KO, 2):
                blocks = []
                for a in range(2):
                    pieces = []
                    for b in range(2):
                        v = back_ref[slot_ref[(row + a) * KO + k + b]]
                        high = v.astype(BF16).astype(F32)
                        pieces.append(jnp.concatenate([high, v - high], axis=0))
                    blocks.append(jnp.concatenate(pieces, axis=1))
                lhs = jnp.concatenate(blocks, axis=0).astype(BF16)
                part = dot(lhs, square(w_ref, row, k), ((1,), (1,)))
                total = part if total is None else total + part
            total_ref[pl.ds(i * FLD, FLD), :] = total[0:4, 0:B] + total[4:8, 0:B]
            total_ref[pl.ds((i + 1) * FLD, FLD), :] = total[8:12, B:] + total[12:16, B:]
        for b in range(GRP):
            ms[pl.ds(b * PITCH, LA - 1), :] = mix_ref[:, block_lanes(step * GRP + b)].astype(F32)
        fields = [total_ref[pl.ds(f, GRP, stride=FLD), :] for f in range(FLD)]

        def load(level):
            v = coef_ref[0, level] * fields[0]
            for f in range(1, FLD):
                v = v + coef_ref[f, level] * fields[f]
            return v

        def emit(level, v):
            steps_ref[pl.ds(level, GRP, stride=PITCH), :] = v

        sweep_levels(load, lambda l: level_rows(ms, l), emit)
        for b in range(GRP):
            out_ref[:, block_lanes(step * GRP + b)] = steps_ref[pl.ds(b * PITCH, LA), :]

    def work(pair, carry):
        for half in range(2):
            w_copy(2 * pair + half).wait()
        for half in range(2):
            one(2 * pair + half)
        for half in range(2):
            out_copy(2 * pair + half).start()
        return carry

    lax.fori_loop(0, STEPS // 2, work, 0)
    for s in range(STEPS):
        out_copy(s).wait()


def atm_adjoint(slots, coef, back, mix, w):
    return pl.pallas_call(
        atm_adjoint_kernel,
        in_specs=[SMEM, SMEM, VMEM, VMEM, ANY],
        out_specs=ANY,
        out_shape=f32(LA, NBA * B),
        scratch_shapes=[
            pltpu.VMEM((NBA * KO, B, B), BF16),
            pltpu.VMEM((GRP * PITCH, B), F32),
            pltpu.VMEM((GRP * FLD, B), F32),
            pltpu.VMEM((GRP * PITCH, B), F32),
            pltpu.VMEM((LA, NBA * B), F32),
            pltpu.SemaphoreType.DMA((3, STEPS)),
        ],
        compiler_params=params(24),
        name="atm_adjoint",
    )(slots, coef, back, mix, in_hbm(w))


def rows_kernel(a_hbm, t_hbm, m_hbm, low_ref, high_ref, a_ref, t_ref, m_ref, sems):
    copies = []
    for i, r in enumerate((0, OY - 8)):
        rows = pl.ds(r, 8)
        copies += [
            pltpu.make_async_copy(a_hbm.at[:, rows], a_ref.at[i], sems.at[0, i]),
            pltpu.make_async_copy(t_hbm.at[:, rows], t_ref.at[i], sems.at[1, i]),
            pltpu.make_async_copy(m_hbm.at[rows], m_ref.at[i], sems.at[2, i]),
        ]
    for c in copies:
        c.start()
    for c in copies:
        c.wait()
    low_ref[0:LO] = a_ref[0, :, 0:2, :] * m_ref[0, 0:2].astype(F32)
    low_ref[LO:] = t_ref[0, :, 0:2, :]
    high_ref[0:LO] = a_ref[1, :, 6:8, :] * m_ref[1, 6:8].astype(F32)
    high_ref[LO:] = t_ref[1, :, 6:8, :]


def edge_rows(adjoint, tangent, mask):
    return pl.pallas_call(
        rows_kernel,
        in_specs=[ANY] * 3,
        out_specs=[VMEM, VMEM],
        out_shape=[f32(2 * LO, 2, B), f32(2 * LO, 2, B)],
        scratch_shapes=[
            pltpu.VMEM((2, LO, 8, B), F32),
            pltpu.VMEM((2, LO, 8, B), F32),
            pltpu.VMEM((2, 8, B), jnp.int32),
            pltpu.SemaphoreType.DMA((3, 2)),
        ],
        compiler_params=params(8),
        name="edge_rows",
    )(in_hbm(adjoint), in_hbm(tangent), in_hbm(mask))


def level_lanes(plane):
    return range(min(32, LO - 32 * plane))


def pack_kernel(a_ref, t_ref, mask_ref, north_ref, south_ref, own_ref, east_ref, west_ref):
    sea = mask_ref[...].astype(F32)
    lane = lanes(1)
    part = lane % 4
    for plane in range(PLANES):
        held = []
        for at, x_ref in ((0, a_ref), (LO, t_ref)):
            body = jnp.zeros((OY, B), F32)
            rim = jnp.zeros((2, B), F32)
            for m in level_lanes(plane):
                level = 32 * plane + m
                mine = lane // 4 == m
                body = jnp.where(mine, pltpu.roll(x_ref[level], (4 * m + 2) % B, 1), body)
                edge = jnp.concatenate(
                    [south_ref[at + level, 0:1], north_ref[at + level, 1:2]], axis=0
                )
                rim = jnp.where(mine, pltpu.roll(edge, (4 * m + 2) % B, 1), rim)
            if at == 0:
                body = body * jnp.where(part < 2, edge_mask(sea, part, True), edge_mask(sea, part, False))
            held.append(
                jnp.concatenate([body, rim[0:1], jnp.zeros((6, B), F32), rim[1:2]], axis=0)
            )
        adj, tan = held
        own_ref[0, plane] = adj
        own_ref[1, plane] = tan
        east_ref[plane] = jnp.where(part < 2, adj, pltpu.roll(tan, 2, 1))
        west_ref[plane] = jnp.where(part < 2, pltpu.roll(adj, B - 2, 1), tan)


def edge_mask(sea, part, high):
    first = B - 2 if high else 0
    return jnp.where(part % 2 == 0, sea[:, first : first + 1], sea[:, first + 1 : first + 2])


def pack_columns(adjoint, tangent, mask, north, south):
    return pl.pallas_call(
        pack_kernel,
        out_shape=[f32(2, PLANES, ROWS, B), f32(PLANES, ROWS, B), f32(PLANES, ROWS, B)],
        compiler_params=params(12),
        name="pack_columns",
    )(adjoint, tangent, mask, north, south)


def lateral_table():
    r = lax.broadcasted_iota(jnp.int32, (B, B), 0)
    c = lax.broadcasted_iota(jnp.int32, (B, B), 1)
    near = ((r - c == 1) | (c - r == 1)).astype(F32).astype(BF16)
    return jnp.concatenate([near, near], axis=0)


def swapped(v, part):
    return jnp.where(part == 2, pltpu.roll(v, 1, 1), pltpu.roll(v, B - 1, 1))


def around_rows(v):
    return pltpu.roll(v, 1, 0) + pltpu.roll(v, ROWS - 1, 0)


def ocean_kernel(adjoint, k_ref, ends_ref, pen_ref, x_ref, mask_ref, north_ref, south_ref,
                 own_ref, west_ref, east_ref, *rest):
    if adjoint:
        out_hbm, flux_ref, state, first, fix, out_ref, sem = rest
    else:
        out_hbm, state, first, fix, out_ref, sem = rest
    sea = mask_ref[...].astype(F32)

    state[:, 8:TOP, :] = jnp.zeros((LO + 1, 8, B), F32)
    state[:, TOP + OY : TOP + OY + 8, :] = jnp.zeros((LO + 1, 8, B), F32)
    state[0:LO, TOP - 2 : TOP, :] = north_ref[...]
    state[0:LO, TOP + OY : TOP + OY + 2, :] = south_ref[...]
    state[LO, TOP : TOP + OY] = jnp.zeros((OY, B), F32)

    def fill(level, carry):
        v = x_ref[level]
        state[level, TOP : TOP + OY] = v * sea if adjoint else v
        return carry

    lax.fori_loop(0, LO, fill, 0, unroll=5)

    lane = lanes(1)
    part = lane % 4
    ups, downs = [], []
    for plane in range(PLANES):
        up = jnp.zeros((1, B), F32)
        down = jnp.zeros((1, B), F32)
        for m in level_lanes(plane):
            level = 32 * plane + m
            mine = lane // 4 == m
            if level < LO - 1:
                up = jnp.where(mine, k_ref[level], up)
            if level > 0:
                down = jnp.where(mine, k_ref[level - 1], down)
        ups.append(up)
        downs.append(down)
    own = [own_ref[0, p] for p in range(PLANES)]
    if adjoint:
        outer = [
            jnp.where(part < 2, west_ref[p], pltpu.roll(east_ref[p], 2, 1)) for p in range(PLANES)
        ]
    else:
        outer = [
            jnp.where(part < 2, pltpu.roll(west_ref[p], B - 2, 1), east_ref[p])
            for p in range(PLANES)
        ]

    def vertical(vs, p):
        c = vs[p]
        higher = pltpu.roll(c, B - 4, 1)
        if p + 1 < PLANES:
            higher = jnp.where(lane < B - 4, higher, pltpu.roll(vs[p + 1], B - 4, 1))
        lower = pltpu.roll(c, 4, 1)
        if p > 0:
            lower = jnp.where(lane >= 4, lower, pltpu.roll(vs[p - 1], 4, 1))
        return c + ups[p] * (higher - c) - downs[p] * (c - lower)

    inner = (part == 1) | (part == 2)
    added = [jnp.where(inner, HRATE * swapped(c, part), 0.0) for c in outer]
    for p in range(PLANES):
        c = outer[p]
        from_west = jnp.where(part == 1, pltpu.roll(c, 1, 1), pltpu.roll(own[p], 1, 1))
        from_east = jnp.where(part == 1, pltpu.roll(own[p], B - 1, 1), pltpu.roll(c, B - 1, 1))
        beyond = vertical(outer, p) + HRATE * (from_west + from_east + around_rows(c) - 4.0 * c)
        e = added[p]
        side = HRATE * (pltpu.roll(e, B - 1, 1) + pltpu.roll(e, 1, 1))
        here = vertical(added, p) + HRATE * (around_rows(e) - 4.0 * e + swapped(beyond, part))
        fix[p] = jnp.where(inner, here, side)[0:OY]

    table = lateral_table()
    first[LO] = jnp.zeros((TALL, B), F32)
    row = lax.broadcasted_iota(jnp.int32, (OY + 16, B), 0) + 8
    keep = jnp.where(
        row == TOP - 1, ends_ref[0].astype(F32), jnp.where(row == TOP + OY, ends_ref[1].astype(F32), 1.0)
    )
    wide = lanes(OY)
    edge_lane = (wide < 2) | (wide >= B - 2)

    def out_copy(group):
        part = pl.ds(group * LEVELS, LEVELS)
        return pltpu.make_async_copy(out_ref.at[part], out_hbm.at[part], sem.at[group])

    def step(src, start, count, second):
        rows = pl.ds(start, count)

        def body(group, below):
            base = group * LEVELS
            vs = [src[base + j, rows, :] for j in range(LEVELS + 1)]
            hi, lo = split2(jnp.concatenate(vs[:LEVELS], axis=0))
            side = dot(jnp.concatenate([hi, lo], axis=1), table)
            for j in range(LEVELS):
                level = base + j
                v = vs[j]
                k = jnp.where(level < LO - 1, k_ref[jnp.minimum(level, LO - 2)], 0.0)
                flow = k * (vs[j + 1] - v)
                near = (
                    src[level, pl.ds(start - 1, count), :]
                    + src[level, pl.ds(start + 1, count), :]
                    + side[j * count : (j + 1) * count]
                )
                done = v * (1.0 - 4.0 * HRATE) + (flow - below) + HRATE * near
                if second:
                    shift = (2 * B - 2 - 4 * (level % 32)) % B
                    extra = pltpu.roll(fix[level // 32], shift, 1)
                    done = done + jnp.where(edge_lane, extra, 0.0)
                    out_ref[level] = done
                else:
                    first[level, rows, :] = done * keep
                below = flow
            if second:
                out_copy(group).start()
            return below

        lax.fori_loop(0, LO // LEVELS, body, jnp.zeros((count, B), F32))

    step(state, 8, OY + 16, False)
    step(first, TOP, OY, True)

    if adjoint:
        tall = 32
        for r in range(0, OY, tall):
            rows = pl.ds(r, tall)

            def project(level, sums):
                v = out_ref[level, rows, :]
                return tuple(s + pen_ref[f, level] * v for f, s in enumerate(sums))

            sums = lax.fori_loop(
                0, LO, project, tuple(jnp.zeros((tall, B), F32) for _ in range(FLD)), unroll=5
            )
            for f in range(FLD):
                flux_ref[rows, f * B : (f + 1) * B] = sums[f]
    for group in range(LO // LEVELS):
        out_copy(group).wait()


def ocean_steps(adjoint, k, ends, pen, x, mask, north, south, own, west, east):
    at = 0 if adjoint else 1
    rim = pl.BlockSpec((LO, 2, B), lambda i: (at, 0, 0))
    full = lambda *shape: pl.BlockSpec(shape, lambda i: (0,) * len(shape))
    shapes = [pltpu.HBM((LO, OY, B), F32)]
    outs = [ANY]
    if adjoint:
        shapes.append(f32(OY, FLD * B))
        outs.append(full(OY, FLD * B))
    return pl.pallas_call(
        functools.partial(ocean_kernel, adjoint),
        grid=(1,),
        in_specs=[
            SMEM,
            SMEM,
            SMEM,
            full(LO, OY, B),
            full(OY, B),
            rim,
            rim,
            pl.BlockSpec((1, PLANES, ROWS, B), lambda i: (at, 0, 0, 0)),
            full(PLANES, ROWS, B),
            full(PLANES, ROWS, B),
        ],
        out_specs=outs,
        out_shape=shapes,
        scratch_shapes=[
            pltpu.VMEM((LO + 1, TALL, B), F32),
            pltpu.VMEM((LO + 1, TALL, B), F32),
            pltpu.VMEM((PLANES, OY, B), F32),
            pltpu.VMEM((LO, OY, B), F32),
            pltpu.SemaphoreType.DMA((LO // LEVELS,)),
        ],
        compiler_params=params(24),
        cost_estimate=cost(6),
        name="ocean_adjoint" if adjoint else "ocean_tangent",
    )(k, ends, pen, x, mask, north, south, own, west, east)


def answer_kernel(msg_ref, flux_ref, out_hbm, out_ref, sems):
    quarter = DEV // 4
    gh, gl = split2(flux_ref[...])
    table = jnp.concatenate([gh, gl], axis=0)
    want = lax.broadcasted_iota(jnp.int32, (quarter, B), 1) % OY + 1
    size = quarter * CAP * FLD
    copies = []
    for q in range(4):
        labels = msg_ref[pl.ds(q * quarter * MSG + MSG - 1, quarter, stride=MSG), :].astype(jnp.int32)
        pick = jnp.concatenate(
            [(labels[:, c : c + 1] == want).astype(F32) for c in range(CAP)], axis=0
        ).astype(BF16)
        rows = dot(pick, table)
        for c in range(CAP):
            for f in range(FLD):
                at = pl.ds(q * size + c * FLD + f, quarter, stride=CAP * FLD)
                out_ref[at, :] = rows[c * quarter : (c + 1) * quarter, f * B : (f + 1) * B]
        part = pl.ds(q * size, size)
        copies.append(pltpu.make_async_copy(out_ref.at[part], out_hbm.at[part], sems.at[q]))
        copies[-1].start()
    for c in copies:
        c.wait()


def answer(msg, flux):
    return pl.pallas_call(
        answer_kernel,
        in_specs=[VMEM, VMEM],
        out_specs=ANY,
        out_shape=pltpu.HBM((DEV * CAP * FLD, B), F32),
        scratch_shapes=[pltpu.VMEM((DEV * CAP * FLD, B), F32), pltpu.SemaphoreType.DMA((4,))],
        compiler_params=params(12),
        cost_estimate=cost(2.5),
        name="answer",
    )(msg, flux)


def collect_kernel(msg_ref, flux_ref, outer_ref, low_ref, high_ref):
    last = msg_ref[pl.ds(MSG - 1, DEV, stride=MSG), :]
    labels = last.T.astype(jnp.int32)
    rows = lax.broadcasted_iota(jnp.int32, (OY, DEV), 0) + 1

    def picked(at):
        return (labels[at : at + 1, :] == rows).astype(F32).astype(BF16)

    lane = lanes(DEV)
    first_lot = lane < 4 * FLD
    total = jnp.zeros((OY, FLD * B), F32)
    outer = jnp.zeros((OY, B), F32)
    for c in range(CAP):
        pick = picked(c)
        data = jnp.concatenate(
            [msg_ref[pl.ds(c * FLD + f, DEV, stride=MSG), :] for f in range(FLD)], axis=1
        )
        dh, dl = split2(data)
        total = total + dot(jnp.concatenate([pick, pick], axis=1), jnp.concatenate([dh, dl], axis=0))
        piece = jnp.where(first_lot, pltpu.roll(last, (2 * B - PIECES - 16 * c) % B, 1), 0.0)
        west = jnp.where(lane % 4 < 2, piece, 0.0)
        wh, wl = split2(west)
        eh, el = split2(piece - west)
        west_pick, east_pick = picked(4 + c), picked(8 + c)
        outer = outer + dot(
            jnp.concatenate([west_pick, west_pick, east_pick, east_pick], axis=1),
            jnp.concatenate([wh, wl, eh, el], axis=0),
        )
    outer_ref[...] = outer
    for f in range(FLD):
        v = total[:, f * B : (f + 1) * B]
        flux_ref[f] = v
        low_ref[f] = v[0:2]
        high_ref[f] = v[OY - 2 : OY]
    low_ref[FLD] = outer[0:2]
    high_ref[FLD] = outer[OY - 2 : OY]


def collect(msg):
    return pl.pallas_call(
        collect_kernel,
        out_shape=[f32(FLD, OY, B), f32(OY, B), f32(FLD + 1, 2, B), f32(FLD + 1, 2, B)],
        compiler_params=params(12),
        cost_estimate=cost(1.6),
        name="collect",
    )(msg)


def circular(own, north, south):
    return jnp.concatenate([own, south, jnp.zeros((ROWS - OY - 4, B), F32), north], axis=0)


def apply_flux_kernel(
    coef_ref, ends_ref, x_ref, mask_ref, flux_ref, outer_ref, north_ref, south_ref,
    out_hbm, terms, out_ref, sems
):
    lane = lanes(1)
    part = lane % 4
    planes = [circular(flux_ref[f], north_ref[f], south_ref[f]) for f in range(FLD)]
    own = jnp.zeros((ROWS, B), F32)
    for f in range(FLD):
        own = jnp.where(lane // 4 == f, pltpu.roll(planes[f], 4 * f + 2, 1), own)
    outer = circular(outer_ref[...], north_ref[FLD], south_ref[FLD])
    from_west = jnp.where(part == 1, pltpu.roll(outer, 1, 1), pltpu.roll(own, 1, 1))
    from_east = jnp.where(part == 1, pltpu.roll(own, B - 1, 1), pltpu.roll(outer, B - 1, 1))
    beyond = from_west + from_east + around_rows(outer) - 4.0 * outer
    outer, beyond = swapped(outer, part), swapped(beyond, part)
    ring = lax.broadcasted_iota(jnp.int32, (ROWS, B), 0)
    keep = jnp.where(
        ring == ROWS - 1, ends_ref[0].astype(F32), jnp.where(ring == OY, ends_ref[1].astype(F32), 1.0)
    )
    wide = lanes(ROWS)

    def laplace(v, cols, f):
        edge = pltpu.roll(cols, B - 2 - 4 * f, 1)
        side = jnp.where(wide == 0, edge, pltpu.roll(v, 1, 1)) + jnp.where(
            wide == B - 1, edge, pltpu.roll(v, B - 1, 1)
        )
        return side + around_rows(v) - 4.0 * v

    for f in range(FLD):
        v = planes[f]
        once = keep * laplace(v, outer, f)
        twice = laplace(once, beyond, f)
        terms[f] = v[0:OY]
        terms[FLD + f] = once[0:OY]
        terms[2 * FLD + f] = twice[0:OY]

    tall = 32
    copies = []
    for i in range(OY // tall):
        rows = pl.ds(i * tall, tall)
        sea = mask_ref[rows, :].astype(F32)
        held = [terms[j, rows, :] for j in range(3 * FLD)]

        def one(level, carry):
            v = x_ref[level, rows, :]
            for j in range(3 * FLD):
                v = v + coef_ref[j, level] * held[j]
            out_ref[level, rows, :] = v * sea
            return carry

        lax.fori_loop(0, LO, one, 0, unroll=5)
        copies.append(pltpu.make_async_copy(out_ref.at[:, rows], out_hbm.at[:, rows], sems.at[i]))
        copies[-1].start()
    for c in copies:
        c.wait()


def apply_flux(coefs, ends, x, mask, flux, outer, north, south):
    return pl.pallas_call(
        apply_flux_kernel,
        in_specs=[SMEM, SMEM] + [VMEM] * 6,
        out_specs=ANY,
        out_shape=f32(LO, OY, B),
        scratch_shapes=[
            pltpu.VMEM((3 * FLD, OY, B), F32),
            pltpu.VMEM((LO, OY, B), F32),
            pltpu.SemaphoreType.DMA((2,)),
        ],
        compiler_params=params(16),
        name="apply_flux",
    )(coefs, ends, x, mask, flux, outer, north, south)


def swap_rows(low_rows, high_rows):
    count = lax.axis_size("face")
    south_going = [(i, i + 1) for i in range(count - 1)]
    north_going = [(i + 1, i) for i in range(count - 1)]
    north = lax.ppermute(high_rows, "face", south_going)
    south = lax.ppermute(low_rows, "face", north_going)
    return north, south


def swap_columns(for_east, for_west):
    count = lax.axis_size("tile")
    east_going = [(i, (i + 1) % count) for i in range(count)]
    west_going = [((i + 1) % count, i) for i in range(count)]
    west = lax.ppermute(for_east, "tile", east_going)
    east = lax.ppermute(for_west, "tile", west_going)
    return west, east


def exchange(rows):
    return lax.all_to_all(rows, ("face", "tile"), split_axis=0, concat_axis=0, tiled=True)


def mix_levels(v, k):
    flow = k[None, :] * (v[:, 1:] - v[:, :-1])
    return v + jnp.pad(flow, ((0, 0), (0, 1))) - jnp.pad(flow, ((0, 0), (1, 0)))


def local(
    atm_tangent,
    atm_mixing,
    flux_coef,
    remap_weight,
    target_device,
    target_row,
    ocean_tangent,
    ocean_mixing,
    penetration,
    sea_mask,
    ocean_adjoint,
):
    face = lax.axis_index("face")
    ends = jnp.stack([face > 0, face < lax.axis_size("face") - 1]).astype(jnp.int32)
    pen = penetration.T
    north, south = swap_rows(*edge_rows(ocean_adjoint, ocean_tangent, sea_mask))
    pair = surface_flux(flux_coef, atm_tangent, atm_mixing)
    pair, north, south = lax.optimization_barrier((pair, north, south))
    own, for_east, for_west = pack_columns(ocean_adjoint, ocean_tangent, sea_mask, north, south)
    pair, for_east, for_west = lax.optimization_barrier((pair, for_east, for_west))
    west, east = swap_columns(for_east, for_west)
    sent, slots = remap(
        lax.axis_size("tile"), target_device.T, target_row.T, pair, remap_weight
    )
    sent, west, east = lax.optimization_barrier((sent, west, east))
    arrived = exchange(sent.reshape(DEV, 1, MSG * B)).reshape(DEV * MSG, B)
    ocean_backward, flux_adjoint = ocean_steps(
        True, ocean_mixing, ends, pen, ocean_adjoint, sea_mask, north, south, own, west, east
    )
    (stepped,) = ocean_steps(
        False, ocean_mixing, ends, pen, ocean_tangent, sea_mask, north, south, own, west, east
    )
    flux_adjoint, stepped = lax.optimization_barrier((flux_adjoint, stepped))
    returned = exchange(answer(arrived, flux_adjoint).reshape(DEV, CAP, FLD, B))
    pen_1 = mix_levels(pen, ocean_mixing)
    pen_2 = mix_levels(pen_1, ocean_mixing)
    coefs = jnp.concatenate([pen_2, (2.0 * HRATE) * pen_1, (HRATE * HRATE) * pen], axis=0)
    flux, outer, low, high = collect(arrived)
    f_north, f_south = swap_rows(low, high)
    ocean_forward = apply_flux(coefs, ends, stepped, sea_mask, flux, outer, f_north, f_south)
    atm = atm_adjoint(
        slots, flux_coef, returned.reshape(DEV * CAP, FLD, B), atm_mixing, remap_weight
    )
    return ocean_forward, ocean_backward, atm


def solution(mesh):
    placed = (
        P(None, ("face", "tile")),
        P(None, ("face", "tile")),
        P(),
        P(("face", "tile"), None, None),
        P(("face", "tile"), None),
        P(("face", "tile"), None),
        P(None, "face", "tile"),
        P(),
        P(),
        P("face", "tile"),
        P(None, "face", "tile"),
    )
    return jax.shard_map(
        local,
        mesh=mesh,
        in_specs=placed,
        out_specs=(P(None, "face", "tile"), P(None, "face", "tile"), P(None, ("face", "tile"))),
        check_vma=False,
    )
```

```python
import functools

import jax
import jax.numpy as jnp
from jax import lax
from jax.experimental import pallas as pl
from jax.experimental.pallas import tpu as pltpu
from jax.sharding import PartitionSpec as P

ATM_SWEEPS = 4
HRATE = 0.1
LA = 64
LO = 75
FLD = 4
B = 128
NBA = 64
KO = 4
OY = 64
CAP = 4
DEV = 128
MSG = CAP * FLD + 1
PIECES = 64
LOT = KO * FLD + 1
GRP = 8
STEPS = NBA // GRP
PLANES = 3
ROWS = 72
TOP = 16
TALL = 96
LEVELS = 25
F32 = jnp.float32
BF16 = jnp.bfloat16
MIB = 1024 * 1024
SMEM = pl.BlockSpec(memory_space=pltpu.SMEM)
VMEM = pl.BlockSpec(memory_space=pltpu.VMEM)
ANY = pl.BlockSpec(memory_space=pl.ANY)
PITCH = LA + 1


def params(mib):
    return pltpu.CompilerParams(vmem_limit_bytes=mib * MIB)


def cost(us):
    return pl.CostEstimate(
        flops=int(us * 300000000), bytes_accessed=int(us * 900000), transcendentals=0
    )


def in_hbm(v):
    return pltpu.with_memory_space_constraint(v, pltpu.HBM)


def f32(*shape):
    return jax.ShapeDtypeStruct(shape, F32)


def split2(v):
    hi = v.astype(BF16)
    return hi, (v - hi.astype(F32)).astype(BF16)


def dot(a, b, dims=((1,), (0,))):
    return lax.dot_general(a, b, (dims, ((), ())), preferred_element_type=F32)


def lanes(rows):
    return lax.broadcasted_iota(jnp.int32, (rows, B), 1)


def sweep_levels(load, mixing, emit):
    values = [{} for _ in range(ATM_SWEEPS + 1)]
    flows = [{} for _ in range(ATM_SWEEPS)]
    mix = {}
    for t in range(LA + ATM_SWEEPS):
        if t < LA:
            values[0][t] = load(t)
            if t < LA - 1:
                mix[t] = mixing(t)
        for s in range(ATM_SWEEPS):
            l = t - 1 - s
            if not 0 <= l < LA:
                continue
            v = values[s][l]
            done = v
            if l < LA - 1:
                flows[s][l] = mix[l] * (values[s][l + 1] - v)
                done = done + flows[s][l]
            if l > 0:
                done = done - flows[s][l - 1]
            values[s + 1][l] = done
            if s == ATM_SWEEPS - 1:
                emit(l, done)


def level_rows(ref, level):
    return ref[pl.ds(level, GRP, stride=PITCH), :]


def block_lanes(block):
    return pl.ds(pl.multiple_of(block * B, B), B)


def square(w_ref, block, k):
    at = block * KO + k
    return jnp.concatenate(
        [
            jnp.concatenate([w_ref[at], w_ref[at + 1]], axis=1),
            jnp.concatenate([w_ref[at + KO], w_ref[at + KO + 1]], axis=1),
        ],
        axis=0,
    )


def surface_flux_kernel(coef_ref, x_hbm, mix_hbm, out_ref, x_ref, mix_ref, xs, ms, sems):
    cols = GRP * B

    def x_copy(s):
        part = pl.ds(s * cols, cols)
        return pltpu.make_async_copy(x_hbm.at[:, part], x_ref.at[:, part], sems.at[0, s])

    def mix_copy(s):
        part = pl.ds(s * cols, cols)
        return pltpu.make_async_copy(mix_hbm.at[:, part], mix_ref.at[:, part], sems.at[1, s])

    for s in range(STEPS):
        x_copy(s).start()
        mix_copy(s).start()

    def one(step):
        for b in range(GRP):
            at = block_lanes(step * GRP + b)
            xs[step % 2, pl.ds(b * PITCH, LA), :] = x_ref[:, at]
            ms[step % 2, pl.ds(b * PITCH, LA - 1), :] = mix_ref[:, at].astype(F32)
        sums = [None] * FLD

        def emit(level, v):
            for f in range(FLD):
                term = coef_ref[f, level] * v
                sums[f] = term if sums[f] is None else sums[f] + term

        sweep_levels(
            lambda l: level_rows(xs.at[step % 2], l), lambda l: level_rows(ms.at[step % 2], l), emit
        )
        for f in range(FLD):
            high = sums[f].astype(BF16).astype(F32)
            at = step * GRP * 2 * FLD + f
            out_ref[pl.ds(at, GRP, stride=2 * FLD), :] = high
            out_ref[pl.ds(at + FLD, GRP, stride=2 * FLD), :] = sums[f] - high

    def work(pair, carry):
        for half in range(2):
            x_copy(2 * pair + half).wait()
            mix_copy(2 * pair + half).wait()
        for half in range(2):
            one(2 * pair + half)
        return carry

    lax.fori_loop(0, STEPS // 2, work, 0)


def surface_flux(coef, x, mix):
    return pl.pallas_call(
        surface_flux_kernel,
        in_specs=[SMEM, ANY, ANY],
        out_specs=VMEM,
        out_shape=f32(NBA * 2 * FLD, B),
        scratch_shapes=[
            pltpu.VMEM((LA, NBA * B), F32),
            pltpu.VMEM((LA - 1, NBA * B), BF16),
            pltpu.VMEM((2, GRP * PITCH, B), F32),
            pltpu.VMEM((2, GRP * PITCH, B), F32),
            pltpu.SemaphoreType.DMA((2, STEPS)),
        ],
        compiler_params=params(12),
        name="surface_flux",
    )(coef, in_hbm(x), in_hbm(mix))


def columns_of(rows):
    count, length = rows.shape
    wide = jnp.concatenate([rows, jnp.zeros((count, B - length), F32)], axis=1)
    return jnp.concatenate([wide, jnp.zeros((B - count, B), F32)], axis=0).T[0:length]


def label_rows(td_ref, tr_ref, parts, tiles):
    dev = td_ref[...]
    dev_cols = columns_of(dev.astype(F32))
    row_cols = columns_of(tr_ref[...].astype(F32) + 1.0)
    east = dev // tiles * tiles + (dev + 1) % tiles
    west = dev // tiles * tiles + (dev + tiles - 1) % tiles
    lane = lanes(NBA)
    earlier = (
        lax.broadcasted_iota(jnp.int32, (NBA, NBA), 1) < lax.broadcasted_iota(jnp.int32, (NBA, NBA), 0)
    )
    owner = lax.broadcasted_iota(jnp.int32, (DEV, NBA), 0)
    total = jnp.zeros((DEV, B), F32)
    for k in range(KO):
        mine = dev_cols[:, k : k + 1]
        same = jnp.zeros((NBA, NBA), F32)
        for other in range(KO):
            same = same + (mine == dev[other : other + 1].astype(F32)).astype(F32)
        place = jnp.sum(jnp.where(earlier, same, 0.0), axis=1, keepdims=True).astype(jnp.int32)
        label = row_cols[:, k : k + 1]
        piece = jnp.zeros((NBA, B), F32)
        for f in range(FLD):
            v = parts[pl.ds(k * FLD + f, NBA, stride=LOT), :]
            piece = jnp.where(lane // 4 == f, pltpu.roll(v, 4 * f + 2, 1), piece)
        piece = piece + pltpu.roll(piece, 16, 1)
        piece = pltpu.roll(piece + pltpu.roll(piece, 32, 1), PIECES, 1)
        piece = jnp.where(lane // 16 == PIECES // 16 + place, piece, 0.0)
        own = jnp.where(lane == place, label, 0.0)
        to_east = jnp.where(lane == 4 + place, label, jnp.where(lane % 4 < 2, piece, 0.0))
        to_west = jnp.where(lane == 8 + place, label, jnp.where(lane % 4 < 2, 0.0, piece))
        picks = [
            (owner == d[k : k + 1]).astype(F32).astype(BF16) for d in (dev, east, west)
        ]
        hi, lo = split2(jnp.concatenate([own, to_east, to_west], axis=0))
        pick = jnp.concatenate(picks, axis=1)
        total = total + dot(pick, hi) + dot(pick, lo)
    return total


def remap_kernel(tiles, td_ref, td_rows, tr_rows, pair_ref, w_ref, out_ref, slot_ref, count, parts):
    out_ref[...] = jnp.zeros_like(out_ref)

    def clear(d, c):
        count[d] = 0
        return c

    lax.fori_loop(0, DEV, clear, 0, unroll=8)
    upper = lax.broadcasted_iota(jnp.int32, (4 * FLD, B), 0) < 2 * FLD

    def work(step, carry):
        for i in range(0, GRP, 2):
            row = step * GRP + i
            both = pair_ref[pl.ds(pl.multiple_of(row * 2 * FLD, 4 * FLD), 4 * FLD), :]
            lhs = jnp.concatenate(
                [jnp.where(upper, both, 0.0), jnp.where(upper, 0.0, both)], axis=1
            ).astype(BF16)
            ats = {}
            for a in range(2):
                for k in range(KO):
                    dev = td_ref[k, row + a]
                    place = count[dev]
                    count[dev] = place + 1
                    slot_ref[(row + a) * KO + k] = dev * CAP + place
                    ats[a, k] = dev * MSG + place * FLD
            for k in range(0, KO, 2):
                moved = dot(lhs, square(w_ref, row, k))
                for a in range(2):
                    total = moved[8 * a : 8 * a + 4] + moved[8 * a + 4 : 8 * a + 8]
                    for b in range(2):
                        half = total[:, b * B : (b + 1) * B]
                        out_ref[pl.ds(ats[a, k + b], FLD), :] = half
                        parts[pl.ds((row + a) * LOT + (k + b) * FLD, FLD), :] = half
        return carry

    lax.fori_loop(0, STEPS, work, 0, unroll=STEPS)
    out_ref[pl.ds(MSG - 1, DEV, stride=MSG), :] = label_rows(td_rows, tr_rows, parts, tiles)


def remap(tiles, td, tr, pair, w):
    return pl.pallas_call(
        functools.partial(remap_kernel, tiles),
        in_specs=[SMEM] + [VMEM] * 4,
        out_specs=[VMEM, SMEM],
        out_shape=[pltpu.HBM((DEV * MSG, B), F32), jax.ShapeDtypeStruct((NBA * KO,), jnp.int32)],
        scratch_shapes=[pltpu.SMEM((DEV,), jnp.int32), pltpu.VMEM((NBA * LOT, B), F32)],
        compiler_params=params(16),
        name="remap",
    )(td, td, tr, pair, w)


def atm_adjoint_kernel(
    slot_ref, coef_ref, back_ref, mix_ref, w_hbm, out_hbm, w_ref, ms, total_ref, steps_ref, out_ref, sems
):
    cols = GRP * B

    def w_copy(s):
        part = pl.ds(s * GRP * KO, GRP * KO)
        return pltpu.make_async_copy(w_hbm.at[part], w_ref.at[part], sems.at[0, s])

    def out_copy(s):
        part = pl.ds(pl.multiple_of(s * cols, cols), cols)
        return pltpu.make_async_copy(out_ref.at[:, part], out_hbm.at[:, part], sems.at[1, s])

    for s in range(STEPS):
        w_copy(s).start()

    def one(step):
        for i in range(0, GRP, 2):
            row = step * GRP + i
            total = None
            for k in range(0, KO, 2):
                blocks = []
                for a in range(2):
                    pieces = []
                    for b in range(2):
                        v = back_ref[slot_ref[(row + a) * KO + k + b]]
                        high = v.astype(BF16).astype(F32)
                        pieces.append(jnp.concatenate([high, v - high], axis=0))
                    blocks.append(jnp.concatenate(pieces, axis=1))
                lhs = jnp.concatenate(blocks, axis=0).astype(BF16)
                part = dot(lhs, square(w_ref, row, k), ((1,), (1,)))
                total = part if total is None else total + part
            total_ref[pl.ds(i * FLD, FLD), :] = total[0:4, 0:B] + total[4:8, 0:B]
            total_ref[pl.ds((i + 1) * FLD, FLD), :] = total[8:12, B:] + total[12:16, B:]
        for b in range(GRP):
            ms[pl.ds(b * PITCH, LA - 1), :] = mix_ref[:, block_lanes(step * GRP + b)].astype(F32)
        fields = [total_ref[pl.ds(f, GRP, stride=FLD), :] for f in range(FLD)]

        def load(level):
            v = coef_ref[0, level] * fields[0]
            for f in range(1, FLD):
                v = v + coef_ref[f, level] * fields[f]
            return v

        def emit(level, v):
            steps_ref[pl.ds(level, GRP, stride=PITCH), :] = v

        sweep_levels(load, lambda l: level_rows(ms, l), emit)
        for b in range(GRP):
            out_ref[:, block_lanes(step * GRP + b)] = steps_ref[pl.ds(b * PITCH, LA), :]

    def work(pair, carry):
        for half in range(2):
            w_copy(2 * pair + half).wait()
        for half in range(2):
            one(2 * pair + half)
        for half in range(2):
            out_copy(2 * pair + half).start()
        return carry

    lax.fori_loop(0, STEPS // 2, work, 0)
    for s in range(STEPS):
        out_copy(s).wait()


def atm_adjoint(slots, coef, back, mix, w):
    return pl.pallas_call(
        atm_adjoint_kernel,
        in_specs=[SMEM, SMEM, VMEM, VMEM, ANY],
        out_specs=ANY,
        out_shape=f32(LA, NBA * B),
        scratch_shapes=[
            pltpu.VMEM((NBA * KO, B, B), BF16),
            pltpu.VMEM((GRP * PITCH, B), F32),
            pltpu.VMEM((GRP * FLD, B), F32),
            pltpu.VMEM((GRP * PITCH, B), F32),
            pltpu.VMEM((LA, NBA * B), F32),
            pltpu.SemaphoreType.DMA((3, STEPS)),
        ],
        compiler_params=params(24),
        name="atm_adjoint",
    )(slots, coef, back, mix, in_hbm(w))


def rows_kernel(a_hbm, t_hbm, m_hbm, low_ref, high_ref, a_ref, t_ref, m_ref, sems):
    copies = []
    for i, r in enumerate((0, OY - 8)):
        rows = pl.ds(r, 8)
        copies += [
            pltpu.make_async_copy(a_hbm.at[:, rows], a_ref.at[i], sems.at[0, i]),
            pltpu.make_async_copy(t_hbm.at[:, rows], t_ref.at[i], sems.at[1, i]),
            pltpu.make_async_copy(m_hbm.at[rows], m_ref.at[i], sems.at[2, i]),
        ]
    for c in copies:
        c.start()
    for c in copies:
        c.wait()
    low_ref[0:LO] = a_ref[0, :, 0:2, :] * m_ref[0, 0:2].astype(F32)
    low_ref[LO:] = t_ref[0, :, 0:2, :]
    high_ref[0:LO] = a_ref[1, :, 6:8, :] * m_ref[1, 6:8].astype(F32)
    high_ref[LO:] = t_ref[1, :, 6:8, :]


def edge_rows(adjoint, tangent, mask):
    return pl.pallas_call(
        rows_kernel,
        in_specs=[ANY] * 3,
        out_specs=[VMEM, VMEM],
        out_shape=[f32(2 * LO, 2, B), f32(2 * LO, 2, B)],
        scratch_shapes=[
            pltpu.VMEM((2, LO, 8, B), F32),
            pltpu.VMEM((2, LO, 8, B), F32),
            pltpu.VMEM((2, 8, B), jnp.int32),
            pltpu.SemaphoreType.DMA((3, 2)),
        ],
        compiler_params=params(8),
        name="edge_rows",
    )(in_hbm(adjoint), in_hbm(tangent), in_hbm(mask))


def level_lanes(plane):
    return range(min(32, LO - 32 * plane))


def pack_kernel(a_ref, t_ref, mask_ref, north_ref, south_ref, own_ref, east_ref, west_ref):
    sea = mask_ref[...].astype(F32)
    lane = lanes(1)
    part = lane % 4
    for plane in range(PLANES):
        held = []
        for at, x_ref in ((0, a_ref), (LO, t_ref)):
            body = jnp.zeros((OY, B), F32)
            rim = jnp.zeros((2, B), F32)
            for m in level_lanes(plane):
                level = 32 * plane + m
                mine = lane // 4 == m
                body = jnp.where(mine, pltpu.roll(x_ref[level], (4 * m + 2) % B, 1), body)
                edge = jnp.concatenate(
                    [south_ref[at + level, 0:1], north_ref[at + level, 1:2]], axis=0
                )
                rim = jnp.where(mine, pltpu.roll(edge, (4 * m + 2) % B, 1), rim)
            if at == 0:
                body = body * jnp.where(part < 2, edge_mask(sea, part, True), edge_mask(sea, part, False))
            held.append(
                jnp.concatenate([body, rim[0:1], jnp.zeros((6, B), F32), rim[1:2]], axis=0)
            )
        adj, tan = held
        own_ref[0, plane] = adj
        own_ref[1, plane] = tan
        east_ref[plane] = jnp.where(part < 2, adj, pltpu.roll(tan, 2, 1))
        west_ref[plane] = jnp.where(part < 2, pltpu.roll(adj, B - 2, 1), tan)


def edge_mask(sea, part, high):
    first = B - 2 if high else 0
    return jnp.where(part % 2 == 0, sea[:, first : first + 1], sea[:, first + 1 : first + 2])


def pack_columns(adjoint, tangent, mask, north, south):
    return pl.pallas_call(
        pack_kernel,
        out_shape=[f32(2, PLANES, ROWS, B), f32(PLANES, ROWS, B), f32(PLANES, ROWS, B)],
        compiler_params=params(12),
        name="pack_columns",
    )(adjoint, tangent, mask, north, south)


def lateral_table():
    r = lax.broadcasted_iota(jnp.int32, (B, B), 0)
    c = lax.broadcasted_iota(jnp.int32, (B, B), 1)
    near = ((r - c == 1) | (c - r == 1)).astype(F32).astype(BF16)
    return jnp.concatenate([near, near], axis=0)


def swapped(v, part):
    return jnp.where(part == 2, pltpu.roll(v, 1, 1), pltpu.roll(v, B - 1, 1))


def around_rows(v):
    return pltpu.roll(v, 1, 0) + pltpu.roll(v, ROWS - 1, 0)


def ocean_kernel(adjoint, k_ref, ends_ref, pen_ref, x_ref, mask_ref, north_ref, south_ref,
                 own_ref, west_ref, east_ref, *rest):
    if adjoint:
        out_hbm, flux_ref, state, first, fix, out_ref, sem = rest
    else:
        out_hbm, state, first, fix, out_ref, sem = rest
    sea = mask_ref[...].astype(F32)

    state[:, 8:TOP, :] = jnp.zeros((LO + 1, 8, B), F32)
    state[:, TOP + OY : TOP + OY + 8, :] = jnp.zeros((LO + 1, 8, B), F32)
    state[0:LO, TOP - 2 : TOP, :] = north_ref[...]
    state[0:LO, TOP + OY : TOP + OY + 2, :] = south_ref[...]
    state[LO, TOP : TOP + OY] = jnp.zeros((OY, B), F32)

    def fill(level, carry):
        v = x_ref[level]
        state[level, TOP : TOP + OY] = v * sea if adjoint else v
        return carry

    lax.fori_loop(0, LO, fill, 0, unroll=5)

    lane = lanes(1)
    part = lane % 4
    ups, downs = [], []
    for plane in range(PLANES):
        up = jnp.zeros((1, B), F32)
        down = jnp.zeros((1, B), F32)
        for m in level_lanes(plane):
            level = 32 * plane + m
            mine = lane // 4 == m
            if level < LO - 1:
                up = jnp.where(mine, k_ref[level], up)
            if level > 0:
                down = jnp.where(mine, k_ref[level - 1], down)
        ups.append(up)
        downs.append(down)
    own = [own_ref[0, p] for p in range(PLANES)]
    if adjoint:
        outer = [
            jnp.where(part < 2, west_ref[p], pltpu.roll(east_ref[p], 2, 1)) for p in range(PLANES)
        ]
    else:
        outer = [
            jnp.where(part < 2, pltpu.roll(west_ref[p], B - 2, 1), east_ref[p])
            for p in range(PLANES)
        ]

    def vertical(vs, p):
        c = vs[p]
        higher = pltpu.roll(c, B - 4, 1)
        if p + 1 < PLANES:
            higher = jnp.where(lane < B - 4, higher, pltpu.roll(vs[p + 1], B - 4, 1))
        lower = pltpu.roll(c, 4, 1)
        if p > 0:
            lower = jnp.where(lane >= 4, lower, pltpu.roll(vs[p - 1], 4, 1))
        return c + ups[p] * (higher - c) - downs[p] * (c - lower)

    inner = (part == 1) | (part == 2)
    added = [jnp.where(inner, HRATE * swapped(c, part), 0.0) for c in outer]
    for p in range(PLANES):
        c = outer[p]
        from_west = jnp.where(part == 1, pltpu.roll(c, 1, 1), pltpu.roll(own[p], 1, 1))
        from_east = jnp.where(part == 1, pltpu.roll(own[p], B - 1, 1), pltpu.roll(c, B - 1, 1))
        beyond = vertical(outer, p) + HRATE * (from_west + from_east + around_rows(c) - 4.0 * c)
        e = added[p]
        side = HRATE * (pltpu.roll(e, B - 1, 1) + pltpu.roll(e, 1, 1))
        here = vertical(added, p) + HRATE * (around_rows(e) - 4.0 * e + swapped(beyond, part))
        fix[p] = jnp.where(inner, here, side)[0:OY]

    table = lateral_table()
    first[LO] = jnp.zeros((TALL, B), F32)
    row = lax.broadcasted_iota(jnp.int32, (OY + 16, B), 0) + 8
    keep = jnp.where(
        row == TOP - 1, ends_ref[0].astype(F32), jnp.where(row == TOP + OY, ends_ref[1].astype(F32), 1.0)
    )
    wide = lanes(OY)
    edge_lane = (wide < 2) | (wide >= B - 2)

    def out_copy(group):
        part = pl.ds(group * LEVELS, LEVELS)
        return pltpu.make_async_copy(out_ref.at[part], out_hbm.at[part], sem.at[group])

    def step(src, start, count, second):
        rows = pl.ds(start, count)

        def body(group, below):
            base = group * LEVELS
            vs = [src[base + j, rows, :] for j in range(LEVELS + 1)]
            hi, lo = split2(jnp.concatenate(vs[:LEVELS], axis=0))
            side = dot(jnp.concatenate([hi, lo], axis=1), table)
            for j in range(LEVELS):
                level = base + j
                v = vs[j]
                k = jnp.where(level < LO - 1, k_ref[jnp.minimum(level, LO - 2)], 0.0)
                flow = k * (vs[j + 1] - v)
                near = (
                    src[level, pl.ds(start - 1, count), :]
                    + src[level, pl.ds(start + 1, count), :]
                    + side[j * count : (j + 1) * count]
                )
                done = v * (1.0 - 4.0 * HRATE) + (flow - below) + HRATE * near
                if second:
                    shift = (2 * B - 2 - 4 * (level % 32)) % B
                    extra = pltpu.roll(fix[level // 32], shift, 1)
                    done = done + jnp.where(edge_lane, extra, 0.0)
                    out_ref[level] = done
                else:
                    first[level, rows, :] = done * keep
                below = flow
            if second:
                out_copy(group).start()
            return below

        lax.fori_loop(0, LO // LEVELS, body, jnp.zeros((count, B), F32))

    step(state, 8, OY + 16, False)
    step(first, TOP, OY, True)

    if adjoint:
        tall = 32
        for r in range(0, OY, tall):
            rows = pl.ds(r, tall)

            def project(level, sums):
                v = out_ref[level, rows, :]
                return tuple(s + pen_ref[f, level] * v for f, s in enumerate(sums))

            sums = lax.fori_loop(
                0, LO, project, tuple(jnp.zeros((tall, B), F32) for _ in range(FLD)), unroll=5
            )
            for f in range(FLD):
                flux_ref[rows, f * B : (f + 1) * B] = sums[f]
    for group in range(LO // LEVELS):
        out_copy(group).wait()


def ocean_steps(adjoint, k, ends, pen, x, mask, north, south, own, west, east):
    at = 0 if adjoint else 1
    rim = pl.BlockSpec((LO, 2, B), lambda i: (at, 0, 0))
    full = lambda *shape: pl.BlockSpec(shape, lambda i: (0,) * len(shape))
    shapes = [pltpu.HBM((LO, OY, B), F32)]
    outs = [ANY]
    if adjoint:
        shapes.append(f32(OY, FLD * B))
        outs.append(full(OY, FLD * B))
    return pl.pallas_call(
        functools.partial(ocean_kernel, adjoint),
        grid=(1,),
        in_specs=[
            SMEM,
            SMEM,
            SMEM,
            full(LO, OY, B),
            full(OY, B),
            rim,
            rim,
            pl.BlockSpec((1, PLANES, ROWS, B), lambda i: (at, 0, 0, 0)),
            full(PLANES, ROWS, B),
            full(PLANES, ROWS, B),
        ],
        out_specs=outs,
        out_shape=shapes,
        scratch_shapes=[
            pltpu.VMEM((LO + 1, TALL, B), F32),
            pltpu.VMEM((LO + 1, TALL, B), F32),
            pltpu.VMEM((PLANES, OY, B), F32),
            pltpu.VMEM((LO, OY, B), F32),
            pltpu.SemaphoreType.DMA((LO // LEVELS,)),
        ],
        compiler_params=params(24),
        cost_estimate=cost(6),
        name="ocean_adjoint" if adjoint else "ocean_tangent",
    )(k, ends, pen, x, mask, north, south, own, west, east)


def answer_kernel(msg_hbm, flux_ref, out_hbm, label_ref, out_ref, sems):
    quarter = DEV // 4
    fetch = pltpu.make_async_copy(msg_hbm.at[:, :, pl.ds((MSG - 1) * B, B)], label_ref, sems.at[4])
    fetch.start()
    gh, gl = split2(flux_ref[...])
    table = jnp.concatenate([gh, gl], axis=0)
    want = lax.broadcasted_iota(jnp.int32, (quarter, B), 1) % OY + 1
    size = quarter * CAP * FLD
    copies = []
    fetch.wait()
    for q in range(4):
        labels = label_ref[pl.ds(q * quarter, quarter), 0, :].astype(jnp.int32)
        pick = jnp.concatenate(
            [(labels[:, c : c + 1] == want).astype(F32) for c in range(CAP)], axis=0
        ).astype(BF16)
        rows = dot(pick, table)
        for c in range(CAP):
            for f in range(FLD):
                at = pl.ds(q * size + c * FLD + f, quarter, stride=CAP * FLD)
                out_ref[at, :] = rows[c * quarter : (c + 1) * quarter, f * B : (f + 1) * B]
        part = pl.ds(q * size, size)
        copies.append(pltpu.make_async_copy(out_ref.at[part], out_hbm.at[part], sems.at[q]))
        copies[-1].start()
    for c in copies:
        c.wait()


def answer(msg, flux):
    return pl.pallas_call(
        answer_kernel,
        in_specs=[ANY, VMEM],
        out_specs=ANY,
        out_shape=pltpu.HBM((DEV * CAP * FLD, B), F32),
        scratch_shapes=[
            pltpu.VMEM((DEV, 1, B), F32),
            pltpu.VMEM((DEV * CAP * FLD, B), F32),
            pltpu.SemaphoreType.DMA((5,)),
        ],
        compiler_params=params(12),
        cost_estimate=cost(2.5),
        name="answer",
    )(msg, flux)


def collect_kernel(msg_ref, flux_ref, outer_ref, low_ref, high_ref):
    last = msg_ref[pl.ds(MSG - 1, DEV, stride=MSG), :]
    labels = last.T.astype(jnp.int32)
    rows = lax.broadcasted_iota(jnp.int32, (OY, DEV), 0) + 1

    def picked(at):
        return (labels[at : at + 1, :] == rows).astype(F32).astype(BF16)

    lane = lanes(DEV)
    first_lot = lane < 4 * FLD
    total = jnp.zeros((OY, FLD * B), F32)
    outer = jnp.zeros((OY, B), F32)
    for c in range(CAP):
        pick = picked(c)
        data = jnp.concatenate(
            [msg_ref[pl.ds(c * FLD + f, DEV, stride=MSG), :] for f in range(FLD)], axis=1
        )
        dh, dl = split2(data)
        total = total + dot(jnp.concatenate([pick, pick], axis=1), jnp.concatenate([dh, dl], axis=0))
        piece = jnp.where(first_lot, pltpu.roll(last, (2 * B - PIECES - 16 * c) % B, 1), 0.0)
        west = jnp.where(lane % 4 < 2, piece, 0.0)
        wh, wl = split2(west)
        eh, el = split2(piece - west)
        west_pick, east_pick = picked(4 + c), picked(8 + c)
        outer = outer + dot(
            jnp.concatenate([west_pick, west_pick, east_pick, east_pick], axis=1),
            jnp.concatenate([wh, wl, eh, el], axis=0),
        )
    outer_ref[...] = outer
    for f in range(FLD):
        v = total[:, f * B : (f + 1) * B]
        flux_ref[f] = v
        low_ref[f] = v[0:2]
        high_ref[f] = v[OY - 2 : OY]
    low_ref[FLD] = outer[0:2]
    high_ref[FLD] = outer[OY - 2 : OY]


def collect(msg):
    return pl.pallas_call(
        collect_kernel,
        out_shape=[f32(FLD, OY, B), f32(OY, B), f32(FLD + 1, 2, B), f32(FLD + 1, 2, B)],
        compiler_params=params(12),
        cost_estimate=cost(1.6),
        name="collect",
    )(msg)


def circular(own, north, south):
    return jnp.concatenate([own, south, jnp.zeros((ROWS - OY - 4, B), F32), north], axis=0)


def apply_flux_kernel(
    coef_ref, ends_ref, x_ref, mask_ref, flux_ref, outer_ref, north_ref, south_ref,
    out_hbm, terms, out_ref, sems
):
    lane = lanes(1)
    part = lane % 4
    planes = [circular(flux_ref[f], north_ref[f], south_ref[f]) for f in range(FLD)]
    own = jnp.zeros((ROWS, B), F32)
    for f in range(FLD):
        own = jnp.where(lane // 4 == f, pltpu.roll(planes[f], 4 * f + 2, 1), own)
    outer = circular(outer_ref[...], north_ref[FLD], south_ref[FLD])
    from_west = jnp.where(part == 1, pltpu.roll(outer, 1, 1), pltpu.roll(own, 1, 1))
    from_east = jnp.where(part == 1, pltpu.roll(own, B - 1, 1), pltpu.roll(outer, B - 1, 1))
    beyond = from_west + from_east + around_rows(outer) - 4.0 * outer
    outer, beyond = swapped(outer, part), swapped(beyond, part)
    ring = lax.broadcasted_iota(jnp.int32, (ROWS, B), 0)
    keep = jnp.where(
        ring == ROWS - 1, ends_ref[0].astype(F32), jnp.where(ring == OY, ends_ref[1].astype(F32), 1.0)
    )
    wide = lanes(ROWS)

    def laplace(v, cols, f):
        edge = pltpu.roll(cols, B - 2 - 4 * f, 1)
        side = jnp.where(wide == 0, edge, pltpu.roll(v, 1, 1)) + jnp.where(
            wide == B - 1, edge, pltpu.roll(v, B - 1, 1)
        )
        return side + around_rows(v) - 4.0 * v

    for f in range(FLD):
        v = planes[f]
        once = keep * laplace(v, outer, f)
        twice = laplace(once, beyond, f)
        terms[f] = v[0:OY]
        terms[FLD + f] = once[0:OY]
        terms[2 * FLD + f] = twice[0:OY]

    tall = 32
    copies = []
    for i in range(OY // tall):
        rows = pl.ds(i * tall, tall)
        sea = mask_ref[rows, :].astype(F32)
        held = [terms[j, rows, :] for j in range(3 * FLD)]

        def one(level, carry):
            v = x_ref[level, rows, :]
            for j in range(3 * FLD):
                v = v + coef_ref[j, level] * held[j]
            out_ref[level, rows, :] = v * sea
            return carry

        lax.fori_loop(0, LO, one, 0, unroll=5)
        copies.append(pltpu.make_async_copy(out_ref.at[:, rows], out_hbm.at[:, rows], sems.at[i]))
        copies[-1].start()
    for c in copies:
        c.wait()


def apply_flux(coefs, ends, x, mask, flux, outer, north, south):
    return pl.pallas_call(
        apply_flux_kernel,
        in_specs=[SMEM, SMEM] + [VMEM] * 6,
        out_specs=ANY,
        out_shape=f32(LO, OY, B),
        scratch_shapes=[
            pltpu.VMEM((3 * FLD, OY, B), F32),
            pltpu.VMEM((LO, OY, B), F32),
            pltpu.SemaphoreType.DMA((2,)),
        ],
        compiler_params=params(16),
        name="apply_flux",
    )(coefs, ends, x, mask, flux, outer, north, south)


def swap_rows(low_rows, high_rows):
    count = lax.axis_size("face")
    south_going = [(i, i + 1) for i in range(count - 1)]
    north_going = [(i + 1, i) for i in range(count - 1)]
    north = lax.ppermute(high_rows, "face", south_going)
    south = lax.ppermute(low_rows, "face", north_going)
    return north, south


def swap_columns(for_east, for_west):
    count = lax.axis_size("tile")
    east_going = [(i, (i + 1) % count) for i in range(count)]
    west_going = [((i + 1) % count, i) for i in range(count)]
    west = lax.ppermute(for_east, "tile", east_going)
    east = lax.ppermute(for_west, "tile", west_going)
    return west, east


def exchange(rows):
    return lax.all_to_all(rows, ("face", "tile"), split_axis=0, concat_axis=0, tiled=True)


def mix_levels(v, k):
    flow = k[None, :] * (v[:, 1:] - v[:, :-1])
    return v + jnp.pad(flow, ((0, 0), (0, 1))) - jnp.pad(flow, ((0, 0), (1, 0)))


def local(
    atm_tangent,
    atm_mixing,
    flux_coef,
    remap_weight,
    target_device,
    target_row,
    ocean_tangent,
    ocean_mixing,
    penetration,
    sea_mask,
    ocean_adjoint,
):
    face = lax.axis_index("face")
    ends = jnp.stack([face > 0, face < lax.axis_size("face") - 1]).astype(jnp.int32)
    pen = penetration.T
    north, south = swap_rows(*edge_rows(ocean_adjoint, ocean_tangent, sea_mask))
    pair = surface_flux(flux_coef, atm_tangent, atm_mixing)
    pair, north, south = lax.optimization_barrier((pair, north, south))
    own, for_east, for_west = pack_columns(ocean_adjoint, ocean_tangent, sea_mask, north, south)
    pair, for_east, for_west = lax.optimization_barrier((pair, for_east, for_west))
    west, east = swap_columns(for_east, for_west)
    sent, slots = remap(
        lax.axis_size("tile"), target_device.T, target_row.T, pair, remap_weight
    )
    sent, west, east = lax.optimization_barrier((sent, west, east))
    messages = exchange(sent.reshape(DEV, 1, MSG * B))
    arrived = messages.reshape(DEV * MSG, B)
    ocean_backward, flux_adjoint = ocean_steps(
        True, ocean_mixing, ends, pen, ocean_adjoint, sea_mask, north, south, own, west, east
    )
    (stepped,) = ocean_steps(
        False, ocean_mixing, ends, pen, ocean_tangent, sea_mask, north, south, own, west, east
    )
    flux_adjoint, stepped = lax.optimization_barrier((flux_adjoint, stepped))
    returned = exchange(answer(messages, flux_adjoint).reshape(DEV, CAP, FLD, B))
    pen_1 = mix_levels(pen, ocean_mixing)
    pen_2 = mix_levels(pen_1, ocean_mixing)
    coefs = jnp.concatenate([pen_2, (2.0 * HRATE) * pen_1, (HRATE * HRATE) * pen], axis=0)
    flux, outer, low, high = collect(arrived)
    f_north, f_south = swap_rows(low, high)
    ocean_forward = apply_flux(coefs, ends, stepped, sea_mask, flux, outer, f_north, f_south)
    atm = atm_adjoint(
        slots, flux_coef, returned.reshape(DEV * CAP, FLD, B), atm_mixing, remap_weight
    )
    return ocean_forward, ocean_backward, atm


def solution(mesh):
    placed = (
        P(None, ("face", "tile")),
        P(None, ("face", "tile")),
        P(),
        P(("face", "tile"), None, None),
        P(("face", "tile"), None),
        P(("face", "tile"), None),
        P(None, "face", "tile"),
        P(),
        P(),
        P("face", "tile"),
        P(None, "face", "tile"),
    )
    return jax.shard_map(
        local,
        mesh=mesh,
        in_specs=placed,
        out_specs=(P(None, "face", "tile"), P(None, "face", "tile"), P(None, ("face", "tile"))),
        check_vma=False,
    )
```
